32 devices in a mesh: ctx: 16 (over z, y, core), head: 2 (over x).
Axes of the slice: x: 2, y: 2, z: 4, core: 2. Of those that a mesh axis runs over, the one named last changes fastest.
Arguments:
- teacher_q: bfloat16 [2, 1024, 8192], P(None, 'ctx'), may hold values from -48 to 48
- teacher_k: bfloat16 [2, 1024, 1024], P(None, 'ctx'), may hold values from -48 to 48
- student_in: bfloat16 [2, 1024, 2048], P(None, 'ctx'), may hold values from -56 to 56
- w_query: bfloat16 [2048, 2048], P('ctx'), may hold values from -0.125 to 0.125
- w_key: bfloat16 [2048, 2048], P('ctx'), may hold values from -0.125 to 0.125
Outputs:
- grad_query: float32 [2048, 2048], P('ctx')
- grad_key: float32 [2048, 2048], P('ctx')
The draws below stay inside these ranges and needn't reach their ends.
All inputs are finite; a program needn't handle non-finite values.
Results may differ from the reference program's by a relative error of at most 0.01.
Values may be sent and summed in bfloat16 or wider, within the bound.
No kernel may reach another device: no remote copies, remote signals or barrier semaphores. Data moves between devices by JAX's collectives and lax.ppermute only.
A program may use at most 64 MiB of HBM per device.

```python
import math
import jax
import jax.numpy as jnp
from jax import lax

DTQ = 8192
DTK = 1024
DS = 2048
HEADS = 64
BATCH = 2
SEQ = 1024


def shaped_values(key, width, factor):
    base_key = jax.random.fold_in(key, 0)
    values = jax.random.truncated_normal(base_key, -4.0, 4.0, (BATCH, SEQ, width), jnp.float32) * factor
    return values


def draw_teacher_q(key, part):
    key = jax.random.fold_in(key, 11)
    return shaped_values(key, DTQ, 0.8).astype(jnp.bfloat16)


def draw_teacher_k(key, part):
    key = jax.random.fold_in(key, 12)
    return shaped_values(key, DTK, 0.8).astype(jnp.bfloat16)


def draw_student_in(key, part):
    key = jax.random.fold_in(key, 13)
    return shaped_values(key, DS, 1.0).astype(jnp.bfloat16)


def levels(own_key, dims, shards, smallest, largest):
    level = 1.0
    for position, shards_of in shards:
        steps = jax.random.uniform(jax.random.fold_in(jax.random.fold_in(own_key, 6), position), (shards_of,), jnp.float32, smallest / len(shards), largest / len(shards))
        level = level * jnp.repeat(jnp.exp(steps), dims[position] // shards_of).reshape((-1,) + (1,) * (len(dims) - 1 - position))
    return level


def bell_draw(key, shape, spread, most, pieces=(), kind=jnp.bfloat16):
    drawn = jax.random.normal(key, shape, jnp.float32) * spread
    if len(pieces) > 0:
        drawn = levels(key, shape, pieces, -0.22, 0.18) * drawn
    return jnp.clip(drawn, min=-most, max=most).astype(kind)


def setup_inputs(seed: int = 0) -> dict:
    keys = jax.random.split(jax.random.key(seed), 6)
    teacher_q = draw_teacher_q(jax.random.fold_in(keys[5], 71), 0)
    teacher_k = draw_teacher_k(jax.random.fold_in(keys[5], 71), 0)
    student_in = draw_student_in(jax.random.fold_in(keys[5], 71), 0)
    w_query = bell_draw(keys[3], (DS, DS), DS ** -0.5, 0.125, ((0, 16),))
    w_key = bell_draw(keys[4], (DS, DS), DS ** -0.5, 0.125, ((0, 16),))
    return {"teacher_q": teacher_q, "teacher_k": teacher_k, "student_in": student_in, "w_query": w_query, "w_key": w_key}


def head_grads(teacher, student, teach_width, stud_width):
    total_rows = teacher.shape[0]
    teach_heads = teacher.reshape(total_rows, HEADS, teach_width).transpose(1, 0, 2)
    stud_heads = student.reshape(total_rows, HEADS, stud_width).transpose(1, 0, 2)

    def one_head(both_parts):
        teach_part, stud_part = both_parts
        teach_scores = jnp.dot(teach_part, teach_part.T, preferred_element_type=jnp.float32) / math.sqrt(teach_width)
        stud_scores = jnp.dot(stud_part, stud_part.T, preferred_element_type=jnp.float32) / math.sqrt(stud_width)
        teach_probs = jax.nn.softmax(teach_scores, axis=1)
        stud_probs = jax.nn.softmax(stud_scores, axis=1)
        difference = (stud_probs - teach_probs).astype(jnp.bfloat16)
        row_term = jnp.dot(difference, stud_part, preferred_element_type=jnp.float32)
        col_term = jnp.dot(difference.T, stud_part, preferred_element_type=jnp.float32)
        return (row_term + col_term) / math.sqrt(stud_width)
    grads = lax.map(one_head, (teach_heads, stud_heads))
    return grads.transpose(1, 0, 2).reshape(total_rows, HEADS * stud_width).astype(jnp.bfloat16)

def reference(teacher_q, teacher_k, student_in, w_query, w_key):
    query_width = DTQ // HEADS
    key_width = DTK // HEADS
    stud_width = DS // HEADS
    grad_query = jnp.zeros((DS, DS), jnp.float32)
    grad_key = jnp.zeros((DS, DS), jnp.float32)
    for index in range(BATCH):
        inputs = student_in[index]
        student_query = jnp.dot(inputs, w_query.T, preferred_element_type=jnp.float32).astype(jnp.bfloat16)
        student_key = jnp.dot(inputs, w_key.T, preferred_element_type=jnp.float32).astype(jnp.bfloat16)
        query_grad = head_grads(teacher_q[index], student_query, query_width, stud_width)
        key_grad = head_grads(teacher_k[index], student_key, key_width, stud_width)
        grad_query = grad_query + jnp.dot(query_grad.T, inputs, preferred_element_type=jnp.float32)
        grad_key = grad_key + jnp.dot(key_grad.T, inputs, preferred_element_type=jnp.float32)
    return (grad_query, grad_key)
```

```python
import functools
import math

import jax
import jax.numpy as jnp
from jax import lax
from jax.experimental import pallas as pl
from jax.experimental.pallas import tpu as pltpu
from jax.sharding import PartitionSpec as P

DTQ = 8192
DTK = 1024
DS = 2048
HEADS = 64
LOG2E = 1.4426950408889634
SPREAD = 80.0


def dot(a, b, ca, cb):
    return lax.dot_general(a, b, (((ca,), (cb,)), ((), ())), preferred_element_type=jnp.float32)


def relation_kernel(
    x_ref, w_ref, t_ref, o_ref, s_ref, et_ref, es_ref, g_ref, *, heads, block
):
    rows, feats = s_ref.shape
    blocks = rows // block
    stud = feats // heads
    teach = t_ref.shape[1] // heads
    widths = (teach, stud)
    factors = tuple(LOG2E / math.sqrt(width) for width in widths)
    aligned = teach % 128 == 0

    def rows_of(index):
        return pl.ds(index * block, block)

    def masked(value, head, width):
        lane = lax.broadcasted_iota(jnp.int32, value.shape, 1)
        keep = (lane >= head * width) & (lane < (head + 1) * width)
        return jnp.where(keep, value, jnp.zeros_like(value))

    def teacher(index, head):
        if aligned:
            part = t_ref.at[:, pl.ds(head * teach, teach)]
            return part[rows_of(index), :], part[...]
        return masked(t_ref[rows_of(index), :], head, teach), t_ref[...]

    def student(index, head):
        return masked(s_ref[rows_of(index), :], head, stud), s_ref[...]

    for index in range(blocks):
        s_ref[rows_of(index), :] = dot(x_ref[rows_of(index), :], w_ref[...], 1, 1).astype(jnp.bfloat16)
    g_ref[...] = jnp.zeros_like(g_ref)

    def norms(ref, width):
        value = ref[...].astype(jnp.float32)
        square = (value * value).astype(jnp.bfloat16)
        column = lax.broadcasted_iota(jnp.int32, (square.shape[1], 128), 0)
        lane = lax.broadcasted_iota(jnp.int32, (square.shape[1], 128), 1)
        member = ((column >= lane * width) & (column < (lane + 1) * width)).astype(jnp.bfloat16)
        total = dot(square, member, 1, 0)
        factor = LOG2E / math.sqrt(width)
        high = jnp.max(total, axis=0, keepdims=True) * (factor * (1 + 2**-6))
        low = jnp.min(total, axis=0, keepdims=True) * (factor * (1 - 2**-6))
        lane = lax.broadcasted_iota(jnp.int32, (1, 128), 1)
        gap = jnp.where(lane < heads, high - low, 0.0)
        tops = [jnp.max(jnp.where(lane == head, high, -jnp.inf)) for head in range(heads)]
        return tops, jnp.max(gap)

    top_t, gap_t = norms(t_ref, teach)
    top_s, gap_s = norms(s_ref, stud)
    safe = jnp.maximum(gap_t, gap_s) < SPREAD

    @pl.when(safe)
    def _():
        for head in range(heads):
            sums = [jnp.zeros((1, rows), jnp.float32) for _ in range(2)]
            for index in range(blocks):
                for k, (own, e_ref, top) in enumerate(
                    ((teacher, et_ref, top_t[head]), (student, es_ref, top_s[head]))
                ):
                    left, right = own(index, head)
                    e = jnp.exp2(dot(left, right, 1, 1) * factors[k] - top)
                    e_ref[rows_of(index), :] = e
                    sums[k] = sums[k] + jnp.sum(e, axis=0, keepdims=True)
            across = [1.0 / total for total in sums]
            down = [jnp.broadcast_to(a, (128, rows)).T[:, :1] for a in across]
            right = masked(s_ref[...], head, stud)
            for index in range(blocks):
                lo = index * block
                h = es_ref[rows_of(index), :] * (down[1][lo : lo + block] + across[1])
                h = h - et_ref[rows_of(index), :] * (down[0][lo : lo + block] + across[0])
                g_ref[rows_of(index), :] += dot(h.astype(jnp.bfloat16), right, 1, 0)

    @pl.when(jnp.logical_not(safe))
    def _():
        for head in range(heads):

            def step(index, carry):
                probs = []
                for k, own in enumerate((teacher, student)):
                    left, right = own(index, head)
                    score = dot(left, right, 1, 1) * (factors[k] / LOG2E)
                    e = jnp.exp(score - jnp.max(score, axis=1, keepdims=True))
                    probs.append(e / jnp.sum(e, axis=1, keepdims=True))
                difference = probs[1] - probs[0]
                right = masked(s_ref[...], head, stud)
                g_ref[rows_of(index), :] += dot(difference.astype(jnp.bfloat16), right, 1, 0)
                left = masked(s_ref[rows_of(index), :], head, stud)
                g_ref[...] += dot(difference.T.astype(jnp.bfloat16), left, 1, 0)
                return carry

            lax.fori_loop(0, blocks, step, 0)

    grad = (g_ref[...] * (1.0 / math.sqrt(stud))).T.astype(jnp.bfloat16)
    columns = math.gcd(x_ref.shape[1], 512)
    for lo in range(0, x_ref.shape[1], columns):
        part = pl.ds(lo, columns)
        o_ref[:, part] = dot(grad, x_ref[:, part], 1, 0).astype(jnp.bfloat16)


def relation(x, w, t, heads):
    rows = x.shape[0]
    feats = w.shape[0]
    block = math.gcd(rows, 256)
    return pl.pallas_call(
        functools.partial(relation_kernel, heads=heads, block=block),
        out_shape=jax.ShapeDtypeStruct(w.shape, jnp.bfloat16),
        in_specs=[pl.BlockSpec(memory_space=pltpu.VMEM)] * 3,
        out_specs=pl.BlockSpec(memory_space=pltpu.VMEM),
        scratch_shapes=[
            pltpu.VMEM((rows, feats), jnp.bfloat16),
            pltpu.VMEM((rows, rows), jnp.float32),
            pltpu.VMEM((rows, rows), jnp.float32),
            pltpu.VMEM((rows, feats), jnp.float32),
        ],
        compiler_params=pltpu.CompilerParams(vmem_limit_bytes=40 * 2**20),
        cost_estimate=pl.CostEstimate(
            flops=2 * rows * rows * 256 * 3 * heads,
            bytes_accessed=2 * (x.size + 2 * w.size + t.size),
            transcendentals=2 * rows * rows * heads,
        ),
        name="relation",
    )(x, w, t)


def by_sequence(ring, teacher_q, teacher_k, student_in, w_query, w_key):
    places = len(ring) * 2
    where = lax.axis_index("ctx")
    index = lax.axis_index("head")
    heads = HEADS // places
    own_q, own_k, own_x = (
        lax.dynamic_index_in_dim(value, index, 0, False) for value in (teacher_q, teacher_k, student_in)
    )

    def regroup(value):
        tokens, width = value.shape
        parts = value.reshape(tokens, places, width // places).transpose(1, 0, 2)
        got = lax.all_to_all(parts, "ctx", 0, 0, tiled=True)
        return got.reshape(places * tokens, width // places)

    tk = regroup(own_k)

    count = len(ring)
    spot = [0] * count
    for position, chip in enumerate(ring):
        spot[chip] = position
    forward, backward, twin = [], [], []
    for position in range(count):
        for core in range(2):
            here = ring[position] * 2 + core
            forward.append((here, ring[(position + 1) % count] * 2 + core))
            backward.append((here, ring[(position - 1) % count] * 2 + core))
            twin.append((here, here ^ 1))
    tokens = own_x.shape[0]
    position = jnp.asarray(spot, jnp.int32)[where // 2]
    chips = jnp.asarray(ring, jnp.int32)
    full = jnp.zeros((places * tokens, own_x.shape[1]), own_x.dtype)

    def place(full, block, step, rows=0):
        chip = chips[(position + step) % count]
        mine = chip * 2 + where % 2
        other = lax.ppermute(block, "ctx", twin)
        full = lax.dynamic_update_slice_in_dim(full, block, mine * tokens + rows, 0)
        return lax.dynamic_update_slice_in_dim(full, other, (mine ^ 1) * tokens + rows, 0)

    full = place(full, own_x, 0)
    ahead = behind = own_x
    for step in range(1, (count + 1) // 2):
        ahead = lax.ppermute(ahead, "ctx", forward)
        behind = lax.ppermute(behind, "ctx", backward)
        full = place(full, ahead, -step)
        full = place(full, behind, step)
    if count % 2 == 0:
        half = tokens // 2
        ahead = lax.ppermute(ahead[:half], "ctx", forward)
        behind = lax.ppermute(behind[half:], "ctx", backward)
        full = place(full, ahead, count // 2)
        full = place(full, behind, count // 2, half)

    tq = regroup(own_q)
    part_k = relation(full, w_key, tk, heads)
    part_q = relation(full, w_query, tq, heads)
    swap = [(0, 1), (1, 0)]

    def both(part):
        other = lax.ppermute(part, "head", swap)
        return part.astype(jnp.float32) + other.astype(jnp.float32)

    return both(part_q), both(part_k)


def score_tile(local_part, key_part, offset, tile_width, head_width):
    key_tile = lax.dynamic_slice_in_dim(key_part, offset, tile_width, 2)
    product = lax.dot_general(
        local_part, key_tile, (((1,), (1,)), ((0,), (0,))), preferred_element_type=jnp.float32
    )
    return product / math.sqrt(head_width)


def by_rows(teacher_q, teacher_k, student_in, w_query, w_key):
    query_width = DTQ // HEADS
    key_width = DTK // HEADS
    stud_width = DS // HEADS
    batch_count = teacher_q.shape[0]
    share = teacher_q.shape[1] // lax.axis_size("head")
    first = lax.axis_index("head") * share
    own_query = lax.dynamic_slice_in_dim(teacher_q, first, share, 1)
    own_key = lax.dynamic_slice_in_dim(teacher_k, first, share, 1)
    own_input = lax.dynamic_slice_in_dim(student_in, first, share, 1)
    teach_query, teach_key = (
        lax.all_to_all(
            own_query.transpose(2, 0, 1), "ctx", split_axis=0, concat_axis=2, tiled=True
        ),
        lax.all_to_all(own_key.transpose(2, 0, 1), "ctx", split_axis=0, concat_axis=2, tiled=True),
    )
    student_rows = lax.all_gather(own_input, "ctx", axis=1, tiled=True)
    row_count = student_rows.shape[1]
    across = (((1,), (2,)), ((), ()))
    stud_query = lax.dot_general(
        w_query, student_rows, across, preferred_element_type=jnp.float32
    ).astype(jnp.bfloat16)
    stud_key = lax.dot_general(
        w_key, student_rows, across, preferred_element_type=jnp.float32
    ).astype(jnp.bfloat16)
    heads_here = stud_query.shape[0] // stud_width
    gathered_all = (
        lax.all_gather(teach_query, "head", axis=2, tiled=True),
        lax.all_gather(teach_key, "head", axis=2, tiled=True),
        lax.all_gather(stud_query, "head", axis=2, tiled=True),
        lax.all_gather(stud_key, "head", axis=2, tiled=True),
    )
    own_all = (teach_query, teach_key, stud_query, stud_key)
    key_count = gathered_all[0].shape[2]
    widths = (query_width, key_width, stud_width, stud_width)
    tile_width = math.gcd(key_count, 512)
    tile_count = key_count // tile_width
    tiles = jnp.arange(tile_count)
    batched = (((2,), (2,)), ((0,), (0,)))
    weight_query = jnp.zeros((heads_here * stud_width, w_query.shape[1]), jnp.float32)
    weight_key = jnp.zeros((heads_here * stud_width, w_key.shape[1]), jnp.float32)
    for index in range(batch_count):
        local_parts = tuple(
            (
                own_all[member][:, index, :].reshape(heads_here, widths[member], row_count)
                for member in range(4)
            )
        )
        key_parts = tuple(
            (
                gathered_all[member][:, index, :].reshape(heads_here, widths[member], key_count)
                for member in range(4)
            )
        )

        def stat_step(state_now, tile_index):
            offset = tile_index * tile_width
            updated = []
            for member in range(4):
                running_max, running_sum = state_now[member]
                scores = score_tile(
                    local_parts[member], key_parts[member], offset, tile_width, widths[member]
                )
                new_max = jnp.maximum(running_max, jnp.max(scores, axis=2))
                running_sum = running_sum * jnp.exp(running_max - new_max) + jnp.sum(
                    jnp.exp(scores - new_max[:, :, None]), axis=2
                )
                updated.append((new_max, running_sum))
            return (tuple(updated), None)

        start_stats = tuple(
            (
                (
                    jnp.full((heads_here, row_count), -jnp.inf, jnp.float32),
                    jnp.zeros((heads_here, row_count), jnp.float32),
                )
                for member in range(4)
            )
        )
        final_stats, unused = lax.scan(stat_step, start_stats, tiles)
        log_totals = tuple(
            (final_stats[member][0] + jnp.log(final_stats[member][1]) for member in range(4))
        )
        zero_terms = jnp.zeros((heads_here, stud_width, row_count), jnp.float32)

        def grad_step(state_now, tile_index):
            offset = tile_index * tile_width
            scores = [
                score_tile(
                    local_parts[member], key_parts[member], offset, tile_width, widths[member]
                )
                for member in range(4)
            ]
            row_probs = [
                jnp.exp(scores[member] - log_totals[member][:, :, None]) for member in range(4)
            ]
            differences = (
                (row_probs[2] - row_probs[0]).astype(jnp.bfloat16),
                (row_probs[3] - row_probs[1]).astype(jnp.bfloat16),
            )
            key_tiles = (
                lax.dynamic_slice_in_dim(key_parts[2], offset, tile_width, 2),
                lax.dynamic_slice_in_dim(key_parts[3], offset, tile_width, 2),
            )
            row_terms = tuple(
                (
                    state_now[member]
                    + lax.dot_general(
                        key_tiles[member],
                        differences[member],
                        batched,
                        preferred_element_type=jnp.float32,
                    )
                    for member in range(2)
                )
            )
            contrib = tuple(
                (
                    lax.dot_general(
                        local_parts[2 + member],
                        differences[member],
                        (((2,), (1,)), ((0,), (0,))),
                        preferred_element_type=jnp.float32,
                    )
                    for member in range(2)
                )
            )
            return (row_terms, contrib)

        sums, pieces = lax.scan(grad_step, (zero_terms, zero_terms), tiles)
        row_query, row_key = sums
        spread = tuple(
            (
                pieces[member].transpose(1, 2, 0, 3).reshape(heads_here, stud_width, key_count)
                for member in range(2)
            )
        )
        col_query, col_key = (
            lax.psum_scatter(
                spread[0].astype(jnp.bfloat16), "head", scatter_dimension=2, tiled=True
            ).astype(jnp.float32),
            lax.psum_scatter(
                spread[1].astype(jnp.bfloat16), "head", scatter_dimension=2, tiled=True
            ).astype(jnp.float32),
        )
        query_grad = (
            ((row_query + col_query) / math.sqrt(stud_width))
            .astype(jnp.bfloat16)
            .reshape(heads_here * stud_width, row_count)
        )
        key_grad = (
            ((row_key + col_key) / math.sqrt(stud_width))
            .astype(jnp.bfloat16)
            .reshape(heads_here * stud_width, row_count)
        )
        weight_query = weight_query + lax.dot_general(
            query_grad,
            student_rows[index],
            (((1,), (0,)), ((), ())),
            preferred_element_type=jnp.float32,
        )
        weight_key = weight_key + lax.dot_general(
            key_grad,
            student_rows[index],
            (((1,), (0,)), ((), ())),
            preferred_element_type=jnp.float32,
        )
    grad_query, grad_key = (
        lax.psum(weight_query.astype(jnp.bfloat16), "head").astype(jnp.float32),
        lax.psum(weight_key.astype(jnp.bfloat16), "head").astype(jnp.float32),
    )
    return (grad_query, grad_key)


def chip_ring(places):
    chips = places // 2
    return [2 * k for k in range(chips // 2)] + [2 * k + 1 for k in reversed(range(chips // 2))]


def solution(mesh):
    placed = (
        P(None, "ctx", None),
        P(None, "ctx", None),
        P(None, "ctx", None),
        P("ctx", None),
        P("ctx", None),
    )
    places = mesh.shape["ctx"]

    def on_device(*args):
        batch, tokens, _ = args[0].shape
        fits = batch == mesh.shape["head"] == 2 and tokens * places <= 1024 and HEADS % places == 0
        if fits and places % 4 == 0:
            return by_sequence(chip_ring(places), *args)
        return by_rows(*args)

    return jax.shard_map(
        on_device,
        mesh=mesh,
        in_specs=placed,
        out_specs=(P("ctx", None), P("ctx", None)),
        check_vma=False,
    )
```

```python
import functools
import math

import jax
import jax.numpy as jnp
from jax import lax
from jax.experimental import pallas as pl
from jax.experimental.pallas import tpu as pltpu
from jax.sharding import PartitionSpec as P

DTQ = 8192
DTK = 1024
DS = 2048
HEADS = 64
LOG2E = 1.4426950408889634
SPREAD = 80.0


def dot(a, b, ca, cb):
    return lax.dot_general(a, b, (((ca,), (cb,)), ((), ())), preferred_element_type=jnp.float32)


def rows_in(index, block):
    return pl.ds(index * block, block)


def masked(value, head, width):
    lane = lax.broadcasted_iota(jnp.int32, value.shape, 1)
    keep = (lane >= head * width) & (lane < (head + 1) * width)
    return jnp.where(keep, value, jnp.zeros_like(value))


def norms(ref, width, heads):
    value = ref[...].astype(jnp.float32)
    square = (value * value).astype(jnp.bfloat16)
    column = lax.broadcasted_iota(jnp.int32, (square.shape[1], 128), 0)
    lane = lax.broadcasted_iota(jnp.int32, (square.shape[1], 128), 1)
    member = ((column >= lane * width) & (column < (lane + 1) * width)).astype(jnp.bfloat16)
    total = dot(square, member, 1, 0)
    factor = LOG2E / math.sqrt(width)
    high = jnp.max(total, axis=0, keepdims=True) * (factor * (1 + 2**-6))
    low = jnp.min(total, axis=0, keepdims=True) * (factor * (1 - 2**-6))
    lane = lax.broadcasted_iota(jnp.int32, (1, 128), 1)
    gap = jnp.where(lane < heads, high - low, 0.0)
    tops = [jnp.max(jnp.where(lane == head, high, -jnp.inf)) for head in range(heads)]
    return tops, jnp.max(gap)


def gradients(t_ref, s_ref, et_ref, es_ref, g_ref, *, heads, chosen, teach, block):
    rows, feats = s_ref.shape
    blocks = rows // block
    stud = feats // heads
    factors = tuple(LOG2E / math.sqrt(width) for width in (teach, stud))
    aligned = teach % 128 == 0

    def teacher(index, head):
        if aligned:
            part = t_ref.at[:, pl.ds(head * teach, teach)]
            return part[rows_in(index, block), :], part[...]
        return masked(t_ref[rows_in(index, block), :], head, teach), t_ref[...]

    def student(index, head):
        return masked(s_ref[rows_in(index, block), :], head, stud), s_ref[...]

    g_ref[...] = jnp.zeros_like(g_ref)
    top_t, gap_t = norms(t_ref, teach, heads)
    top_s, gap_s = norms(s_ref, stud, heads)
    safe = jnp.maximum(gap_t, gap_s) < SPREAD

    @pl.when(safe)
    def _():
        for head in chosen:
            sums = [jnp.zeros((1, rows), jnp.float32) for _ in range(2)]
            for index in range(blocks):
                for k, (own, e_ref, top) in enumerate(
                    ((teacher, et_ref, top_t[head]), (student, es_ref, top_s[head]))
                ):
                    left, right = own(index, head)
                    e = jnp.exp2(dot(left, right, 1, 1) * factors[k] - top)
                    e_ref[rows_in(index, block), :] = e
                    sums[k] = sums[k] + jnp.sum(e, axis=0, keepdims=True)
            across = [1.0 / total for total in sums]
            down = [jnp.broadcast_to(a, (128, rows)).T[:, :1] for a in across]
            right = masked(s_ref[...], head, stud)
            for index in range(blocks):
                lo = index * block
                here = rows_in(index, block)
                h = es_ref[here, :] * (down[1][lo : lo + block] + across[1])
                h = h - et_ref[here, :] * (down[0][lo : lo + block] + across[0])
                g_ref[here, :] += dot(h.astype(jnp.bfloat16), right, 1, 0)

    @pl.when(jnp.logical_not(safe))
    def _():
        for head in chosen:

            def step(index, carry):
                here = rows_in(index, block)
                probs = []
                for k, own in enumerate((teacher, student)):
                    left, right = own(index, head)
                    score = dot(left, right, 1, 1) * (factors[k] / LOG2E)
                    e = jnp.exp(score - jnp.max(score, axis=1, keepdims=True))
                    probs.append(e / jnp.sum(e, axis=1, keepdims=True))
                difference = probs[1] - probs[0]
                right = masked(s_ref[...], head, stud)
                g_ref[here, :] += dot(difference.astype(jnp.bfloat16), right, 1, 0)
                left = masked(s_ref[here, :], head, stud)
                g_ref[...] += dot(difference.T.astype(jnp.bfloat16), left, 1, 0)
                return carry

            lax.fori_loop(0, blocks, step, 0)


def weight_grad(g_ref, x_ref, o_ref, first, stud):
    grad = (g_ref[...] * (1.0 / math.sqrt(stud))).T.astype(jnp.bfloat16)
    grad = grad[first : first + o_ref.shape[0]]
    columns = math.gcd(x_ref.shape[1], 512)
    for lo in range(0, x_ref.shape[1], columns):
        part = pl.ds(lo, columns)
        o_ref[:, part] = dot(grad, x_ref[:, part], 1, 0).astype(jnp.bfloat16)


def key_kernel(*refs, spots, heads, teach, block):
    count = len(spots)
    pieces, refs = refs[:count], refs[count:]
    wq_ref, wk_ref, tk_ref, x_ref, sq_ref, o_ref, sk_ref, t_ref, et_ref, es_ref, g_ref, sems = refs
    places = lax.axis_size("ctx")
    where = lax.axis_index("ctx")
    levels = places // 4
    tokens = x_ref.shape[0] // places
    chip, core = where // 2, where % 2
    level, side = chip // 2, chip % 2
    position = jnp.where(side == 0, level, 2 * levels - 1 - level)
    copies = []
    for number, (piece, (step, twin, offset)) in enumerate(zip(pieces, spots)):
        other = (position + step + 2 * levels) % (2 * levels)
        chip = jnp.where(other < levels, 2 * other, 2 * (2 * levels - 1 - other) + 1)
        row = pl.multiple_of((chip * 2 + (core + twin) % 2) * tokens + offset, piece.shape[0])
        copy = pltpu.make_async_copy(piece, x_ref.at[pl.ds(row, piece.shape[0]), :], sems.at[number])
        copy.start()
        copies.append(copy)
    rows = x_ref.shape[0]
    half = tokens // 2
    for index in range(places):
        part = tk_ref[index * half : (index + 1) * half, :].astype(jnp.float32)
        t_ref[index * tokens : index * tokens + half, :] = part.astype(jnp.bfloat16)
        part = pltpu.roll(part, part.shape[1] // 2, 1)
        t_ref[index * tokens + half : (index + 1) * tokens, :] = part.astype(jnp.bfloat16)
    for copy in copies:
        copy.wait()
    for index in range(rows // block):
        here = rows_in(index, block)
        sq_ref[here, :] = dot(x_ref[here, :], wq_ref[...], 1, 1).astype(jnp.bfloat16)
        sk_ref[here, :] = dot(x_ref[here, :], wk_ref[...], 1, 1).astype(jnp.bfloat16)
    gradients(
        t_ref, sk_ref, et_ref, es_ref, g_ref, heads=heads, chosen=range(heads), teach=teach, block=block
    )
    weight_grad(g_ref, x_ref, o_ref, 0, wk_ref.shape[0] // heads)


def query_kernel(x_ref, s_ref, t_ref, o_ref, et_ref, es_ref, g_ref, *, heads, chosen, block):
    stud = s_ref.shape[1] // heads
    gradients(
        t_ref,
        s_ref,
        et_ref,
        es_ref,
        g_ref,
        heads=heads,
        chosen=chosen,
        teach=t_ref.shape[1] // heads,
        block=block,
    )
    weight_grad(g_ref, x_ref, o_ref, chosen[0] * stud, stud)


def cost(rows, heads):
    return pl.CostEstimate(
        flops=2 * rows * rows * 256 * 3 * heads,
        bytes_accessed=4 * rows * rows,
        transcendentals=2 * rows * rows * heads,
    )


VMEM = pl.BlockSpec(memory_space=pltpu.VMEM)
LIMIT = pltpu.CompilerParams(vmem_limit_bytes=40 * 2**20)


def key_part(pieces, spots, w_query, w_key, tk, heads):
    feats, width = w_key.shape
    rows = 2 * tk.shape[0]
    teach = tk.shape[1] // 2 // heads
    score = pltpu.VMEM((rows, rows), jnp.float32)
    return pl.pallas_call(
        functools.partial(
            key_kernel, spots=tuple(spots), heads=heads, teach=teach, block=math.gcd(rows, 256)
        ),
        out_shape=(
            jax.ShapeDtypeStruct((rows, width), jnp.bfloat16),
            jax.ShapeDtypeStruct((rows, feats), jnp.bfloat16),
            jax.ShapeDtypeStruct((feats, width), jnp.bfloat16),
        ),
        in_specs=[pl.BlockSpec(memory_space=pl.ANY)] * len(pieces) + [VMEM] * 3,
        out_specs=(VMEM, VMEM, VMEM),
        scratch_shapes=[
            pltpu.VMEM((rows, feats), jnp.bfloat16),
            pltpu.VMEM((rows, tk.shape[1]), jnp.bfloat16),
            score,
            score,
            pltpu.VMEM((rows, feats), jnp.float32),
            pltpu.SemaphoreType.DMA((len(pieces),)),
        ],
        compiler_params=LIMIT,
        cost_estimate=cost(rows, heads),
        name="key_type",
    )(*pieces, w_query, w_key, tk)


def query_part(x, s, t, heads, chosen):
    rows, width = x.shape
    stud = s.shape[1] // heads
    score = pltpu.VMEM((rows, rows), jnp.float32)
    return pl.pallas_call(
        functools.partial(query_kernel, heads=heads, chosen=chosen, block=math.gcd(rows, 256)),
        out_shape=jax.ShapeDtypeStruct((len(chosen) * stud, width), jnp.bfloat16),
        in_specs=[VMEM] * 3,
        out_specs=VMEM,
        scratch_shapes=[score, score, pltpu.VMEM(s.shape, jnp.float32)],
        compiler_params=LIMIT,
        cost_estimate=cost(rows, len(chosen)),
        name="query_type",
    )(x, s, t)


def by_sequence(teacher_q, teacher_k, student_in, w_query, w_key):
    places = lax.axis_size("ctx")
    levels = places // 4
    heads = HEADS // places
    index = lax.axis_index("head")
    own_q, own_k, own_x = (
        lax.dynamic_index_in_dim(value, index, 0, False) for value in (teacher_q, teacher_k, student_in)
    )
    tokens = own_x.shape[0]

    ring = [2 * k for k in range(levels)] + [2 * k + 1 for k in reversed(range(levels))]
    count = len(ring)
    forward, backward, twin = [], [], []
    for position in range(count):
        for core in range(2):
            here = ring[position] * 2 + core
            forward.append((here, ring[(position + 1) % count] * 2 + core))
            backward.append((here, ring[position - 1] * 2 + core))
            twin.append((here, here ^ 1))

    pieces, spots = [], []

    def keep(value, step, offset=0):
        pieces.extend((value, lax.ppermute(value, "ctx", twin)))
        spots.extend(((step, 0, offset), (step, 1, offset)))

    keep(own_x, 0)
    ahead = behind = own_x
    for step in range(1, count // 2):
        ahead = lax.ppermute(ahead, "ctx", forward)
        behind = lax.ppermute(behind, "ctx", backward)
        keep(ahead, -step)
        keep(behind, step)
    half = tokens // 2
    ahead = lax.ppermute(ahead[:half], "ctx", forward)
    behind = lax.ppermute(behind[half:], "ctx", backward)
    keep(ahead, -(count // 2))
    keep(behind, count // 2, half)

    width = own_k.shape[1] // places
    parts = own_k.reshape(2, half, places, width).transpose(2, 1, 0, 3).reshape(places, half, 2 * width)
    tk = lax.all_to_all(parts, "ctx", 0, 0, tiled=True).reshape(places * half, 2 * width)
    width = own_q.shape[1] // places
    parts = own_q.reshape(tokens, places, width).transpose(1, 0, 2)
    tq = lax.all_to_all(parts, "ctx", 0, 0, tiled=True).reshape(places * tokens, width)

    x, s, part_k = key_part(pieces, spots, w_query, w_key, tk, heads)
    groups = [tuple(range(lo, lo + heads // 2)) for lo in (0, heads // 2)]

    def both(part):
        other = lax.ppermute(part, "head", [(0, 1), (1, 0)])
        return part.astype(jnp.float32) + other.astype(jnp.float32)

    grad_k = both(part_k)
    grad_q = jnp.concatenate([both(query_part(x, s, tq, heads, chosen)) for chosen in groups])
    return grad_q, grad_k


def score_tile(local_part, key_part, offset, tile_width, head_width):
    key_tile = lax.dynamic_slice_in_dim(key_part, offset, tile_width, 2)
    product = lax.dot_general(
        local_part, key_tile, (((1,), (1,)), ((0,), (0,))), preferred_element_type=jnp.float32
    )
    return product / math.sqrt(head_width)


def by_rows(teacher_q, teacher_k, student_in, w_query, w_key):
    query_width = DTQ // HEADS
    key_width = DTK // HEADS
    stud_width = DS // HEADS
    batch_count = teacher_q.shape[0]
    share = teacher_q.shape[1] // lax.axis_size("head")
    first = lax.axis_index("head") * share
    own_query = lax.dynamic_slice_in_dim(teacher_q, first, share, 1)
    own_key = lax.dynamic_slice_in_dim(teacher_k, first, share, 1)
    own_input = lax.dynamic_slice_in_dim(student_in, first, share, 1)
    teach_query, teach_key = (
        lax.all_to_all(
            own_query.transpose(2, 0, 1), "ctx", split_axis=0, concat_axis=2, tiled=True
        ),
        lax.all_to_all(own_key.transpose(2, 0, 1), "ctx", split_axis=0, concat_axis=2, tiled=True),
    )
    student_rows = lax.all_gather(own_input, "ctx", axis=1, tiled=True)
    row_count = student_rows.shape[1]
    across = (((1,), (2,)), ((), ()))
    stud_query = lax.dot_general(
        w_query, student_rows, across, preferred_element_type=jnp.float32
    ).astype(jnp.bfloat16)
    stud_key = lax.dot_general(
        w_key, student_rows, across, preferred_element_type=jnp.float32
    ).astype(jnp.bfloat16)
    heads_here = stud_query.shape[0] // stud_width
    gathered_all = (
        lax.all_gather(teach_query, "head", axis=2, tiled=True),
        lax.all_gather(teach_key, "head", axis=2, tiled=True),
        lax.all_gather(stud_query, "head", axis=2, tiled=True),
        lax.all_gather(stud_key, "head", axis=2, tiled=True),
    )
    own_all = (teach_query, teach_key, stud_query, stud_key)
    key_count = gathered_all[0].shape[2]
    widths = (query_width, key_width, stud_width, stud_width)
    tile_width = math.gcd(key_count, 512)
    tile_count = key_count // tile_width
    tiles = jnp.arange(tile_count)
    batched = (((2,), (2,)), ((0,), (0,)))
    weight_query = jnp.zeros((heads_here * stud_width, w_query.shape[1]), jnp.float32)
    weight_key = jnp.zeros((heads_here * stud_width, w_key.shape[1]), jnp.float32)
    for index in range(batch_count):
        local_parts = tuple(
            (
                own_all[member][:, index, :].reshape(heads_here, widths[member], row_count)
                for member in range(4)
            )
        )
        key_parts = tuple(
            (
                gathered_all[member][:, index, :].reshape(heads_here, widths[member], key_count)
                for member in range(4)
            )
        )

        def stat_step(state_now, tile_index):
            offset = tile_index * tile_width
            updated = []
            for member in range(4):
                running_max, running_sum = state_now[member]
                scores = score_tile(
                    local_parts[member], key_parts[member], offset, tile_width, widths[member]
                )
                new_max = jnp.maximum(running_max, jnp.max(scores, axis=2))
                running_sum = running_sum * jnp.exp(running_max - new_max) + jnp.sum(
                    jnp.exp(scores - new_max[:, :, None]), axis=2
                )
                updated.append((new_max, running_sum))
            return (tuple(updated), None)

        start_stats = tuple(
            (
                (
                    jnp.full((heads_here, row_count), -jnp.inf, jnp.float32),
                    jnp.zeros((heads_here, row_count), jnp.float32),
                )
                for member in range(4)
            )
        )
        final_stats, unused = lax.scan(stat_step, start_stats, tiles)
        log_totals = tuple(
            (final_stats[member][0] + jnp.log(final_stats[member][1]) for member in range(4))
        )
        zero_terms = jnp.zeros((heads_here, stud_width, row_count), jnp.float32)

        def grad_step(state_now, tile_index):
            offset = tile_index * tile_width
            scores = [
                score_tile(
                    local_parts[member], key_parts[member], offset, tile_width, widths[member]
                )
                for member in range(4)
            ]
            row_probs = [
                jnp.exp(scores[member] - log_totals[member][:, :, None]) for member in range(4)
            ]
            differences = (
                (row_probs[2] - row_probs[0]).astype(jnp.bfloat16),
                (row_probs[3] - row_probs[1]).astype(jnp.bfloat16),
            )
            key_tiles = (
                lax.dynamic_slice_in_dim(key_parts[2], offset, tile_width, 2),
                lax.dynamic_slice_in_dim(key_parts[3], offset, tile_width, 2),
            )
            row_terms = tuple(
                (
                    state_now[member]
                    + lax.dot_general(
                        key_tiles[member],
                        differences[member],
                        batched,
                        preferred_element_type=jnp.float32,
                    )
                    for member in range(2)
                )
            )
            contrib = tuple(
                (
                    lax.dot_general(
                        local_parts[2 + member],
                        differences[member],
                        (((2,), (1,)), ((0,), (0,))),
                        preferred_element_type=jnp.float32,
                    )
                    for member in range(2)
                )
            )
            return (row_terms, contrib)

        sums, pieces = lax.scan(grad_step, (zero_terms, zero_terms), tiles)
        row_query, row_key = sums
        spread = tuple(
            (
                pieces[member].transpose(1, 2, 0, 3).reshape(heads_here, stud_width, key_count)
                for member in range(2)
            )
        )
        col_query, col_key = (
            lax.psum_scatter(
                spread[0].astype(jnp.bfloat16), "head", scatter_dimension=2, tiled=True
            ).astype(jnp.float32),
            lax.psum_scatter(
                spread[1].astype(jnp.bfloat16), "head", scatter_dimension=2, tiled=True
            ).astype(jnp.float32),
        )
        query_grad = (
            ((row_query + col_query) / math.sqrt(stud_width))
            .astype(jnp.bfloat16)
            .reshape(heads_here * stud_width, row_count)
        )
        key_grad = (
            ((row_key + col_key) / math.sqrt(stud_width))
            .astype(jnp.bfloat16)
            .reshape(heads_here * stud_width, row_count)
        )
        weight_query = weight_query + lax.dot_general(
            query_grad,
            student_rows[index],
            (((1,), (0,)), ((), ())),
            preferred_element_type=jnp.float32,
        )
        weight_key = weight_key + lax.dot_general(
            key_grad,
            student_rows[index],
            (((1,), (0,)), ((), ())),
            preferred_element_type=jnp.float32,
        )
    grad_query, grad_key = (
        lax.psum(weight_query.astype(jnp.bfloat16), "head").astype(jnp.float32),
        lax.psum(weight_key.astype(jnp.bfloat16), "head").astype(jnp.float32),
    )
    return (grad_query, grad_key)


def solution(mesh):
    placed = (
        P(None, "ctx", None),
        P(None, "ctx", None),
        P(None, "ctx", None),
        P("ctx", None),
        P("ctx", None),
    )
    places = mesh.shape["ctx"]

    def on_device(*args):
        batch, tokens, _ = args[0].shape
        even = places % 4 == 0 and HEADS % (2 * places) == 0 and tokens % 32 == 0
        if even and batch == mesh.shape["head"] == 2 and tokens * places <= 1024:
            return by_sequence(*args)
        return by_rows(*args)

    return jax.shard_map(
        on_device,
        mesh=mesh,
        in_specs=placed,
        out_specs=(P("ctx", None), P("ctx", None)),
        check_vma=False,
    )
```

```python
import functools
import math

import jax
import jax.numpy as jnp
from jax import lax
from jax.experimental import pallas as pl
from jax.experimental.pallas import tpu as pltpu
from jax.sharding import PartitionSpec as P

DTQ = 8192
DTK = 1024
DS = 2048
HEADS = 64
LOG2E = 1.4426950408889634
SPREAD = 80.0


def dot(a, b, ca, cb):
    return lax.dot_general(a, b, (((ca,), (cb,)), ((), ())), preferred_element_type=jnp.float32)


def turned(number, count):
    return sum(((number >> bit) & 1) * (count >> (bit + 1)) for bit in range(count.bit_length() - 1))


def rows_in(index, block):
    return pl.ds(index * block, block)


def masked(value, head, width):
    lane = lax.broadcasted_iota(jnp.int32, value.shape, 1)
    keep = (lane >= head * width) & (lane < (head + 1) * width)
    return jnp.where(keep, value, jnp.zeros_like(value))


def norms(ref, width, heads):
    value = ref[...].astype(jnp.float32)
    square = (value * value).astype(jnp.bfloat16)
    column = lax.broadcasted_iota(jnp.int32, (square.shape[1], 128), 0)
    lane = lax.broadcasted_iota(jnp.int32, (square.shape[1], 128), 1)
    member = ((column >= lane * width) & (column < (lane + 1) * width)).astype(jnp.bfloat16)
    total = dot(square, member, 1, 0)
    factor = LOG2E / math.sqrt(width)
    high = jnp.max(total, axis=0, keepdims=True) * (factor * (1 + 2**-6))
    low = jnp.min(total, axis=0, keepdims=True) * (factor * (1 - 2**-6))
    lane = lax.broadcasted_iota(jnp.int32, (1, 128), 1)
    gap = jnp.where(lane < heads, high - low, 0.0)
    tops = [jnp.max(jnp.where(lane == head, high, -jnp.inf)) for head in range(heads)]
    return tops, jnp.max(gap)


def gradients(t_ref, s_ref, et_ref, es_ref, g_ref, *, heads, chosen, teach, block):
    rows, feats = s_ref.shape
    blocks = rows // block
    stud = feats // heads
    factors = tuple(LOG2E / math.sqrt(width) for width in (teach, stud))
    aligned = teach % 128 == 0

    def teacher(index, head):
        if aligned:
            part = t_ref.at[:, pl.ds(head * teach, teach)]
            return part[rows_in(index, block), :], part[...]
        return masked(t_ref[rows_in(index, block), :], head, teach), t_ref[...]

    def student(index, head):
        return masked(s_ref[rows_in(index, block), :], head, stud), s_ref[...]

    g_ref[...] = jnp.zeros_like(g_ref)
    top_t, gap_t = norms(t_ref, teach, heads)
    top_s, gap_s = norms(s_ref, stud, heads)
    safe = jnp.maximum(gap_t, gap_s) < SPREAD

    @pl.when(safe)
    def _():
        for head in chosen:
            sums = [jnp.zeros((1, rows), jnp.float32) for _ in range(2)]
            for index in range(blocks):
                for k, (own, e_ref, top) in enumerate(
                    ((teacher, et_ref, top_t[head]), (student, es_ref, top_s[head]))
                ):
                    left, right = own(index, head)
                    e = jnp.exp2(dot(left, right, 1, 1) * factors[k] - top)
                    e_ref[rows_in(index, block), :] = e
                    sums[k] = sums[k] + jnp.sum(e, axis=0, keepdims=True)
            across = [1.0 / total for total in sums]
            down = [jnp.broadcast_to(a, (128, rows)).T[:, :1] for a in across]
            right = masked(s_ref[...], head, stud)
            for index in range(blocks):
                lo = index * block
                here = rows_in(index, block)
                h = es_ref[here, :] * (down[1][lo : lo + block] + across[1])
                h = h - et_ref[here, :] * (down[0][lo : lo + block] + across[0])
                g_ref[here, :] += dot(h.astype(jnp.bfloat16), right, 1, 0)

    @pl.when(jnp.logical_not(safe))
    def _():
        for head in chosen:

            def step(index, carry):
                here = rows_in(index, block)
                probs = []
                for k, own in enumerate((teacher, student)):
                    left, right = own(index, head)
                    score = dot(left, right, 1, 1) * (factors[k] / LOG2E)
                    e = jnp.exp(score - jnp.max(score, axis=1, keepdims=True))
                    probs.append(e / jnp.sum(e, axis=1, keepdims=True))
                difference = probs[1] - probs[0]
                right = masked(s_ref[...], head, stud)
                g_ref[here, :] += dot(difference.astype(jnp.bfloat16), right, 1, 0)
                left = masked(s_ref[here, :], head, stud)
                g_ref[...] += dot(difference.T.astype(jnp.bfloat16), left, 1, 0)
                return carry

            lax.fori_loop(0, blocks, step, 0)


def weight_grad(g_ref, x_ref, o_ref, first, stud):
    grad = (g_ref[...] * (1.0 / math.sqrt(stud))).T.astype(jnp.bfloat16)
    grad = grad[first : first + o_ref.shape[0]]
    columns = math.gcd(x_ref.shape[1], 512)
    for lo in range(0, x_ref.shape[1], columns):
        part = pl.ds(lo, columns)
        o_ref[:, part] = dot(grad, x_ref[:, part], 1, 0).astype(jnp.bfloat16)


def split_kernel(t_ref, o_ref, sems):
    own = t_ref.at[lax.axis_index("head")]
    places, _, width = o_ref.shape
    copies = [
        pltpu.make_async_copy(own.at[:, pl.ds(place * width, width)], o_ref.at[place], sems.at[place])
        for place in range(places)
    ]
    for copy in copies:
        copy.start()
    for copy in copies:
        copy.wait()


def split(t, places):
    return pl.pallas_call(
        split_kernel,
        out_shape=jax.ShapeDtypeStruct((places, t.shape[1], t.shape[2] // places), t.dtype),
        in_specs=[HBM],
        out_specs=VMEM,
        scratch_shapes=[pltpu.SemaphoreType.DMA((places,))],
        name="split",
    )(t)


def key_kernel(*refs, spots, heads, teach, block):
    count = len(spots)
    pieces, refs = refs[:count], refs[count:]
    wq_hbm, wk_hbm, own_ref, twin_ref, x_hbm, sq_hbm, o_ref, *refs = refs
    x_ref, sq_ref, wq_ref, wk_ref, sk_ref, t_ref, et_ref, es_ref, g_ref, sems = refs
    places = lax.axis_size("ctx")
    where = lax.axis_index("ctx")
    levels = places // 4
    rows = x_ref.shape[0]
    tokens = rows // places
    chip, core = where // 2, where % 2
    level, side = chip // 2, chip % 2
    position = jnp.where(side == 0, level, 2 * levels - 1 - level)
    copies = []
    for number, (piece, (step, twin, offset)) in enumerate(zip(pieces, spots)):
        other = (position + step + 2 * levels) % (2 * levels)
        other = jnp.where(other < levels, 2 * other, 2 * (2 * levels - 1 - other) + 1)
        row = pl.multiple_of((other * 2 + (core + twin) % 2) * tokens + offset, piece.shape[0])
        target = x_ref.at[pl.ds(row, piece.shape[0]), :]
        copies.append(pltpu.make_async_copy(piece, target, sems.at[number]))
    for number, (source, target) in enumerate(((wq_hbm, wq_ref), (wk_hbm, wk_ref))):
        copies.append(pltpu.make_async_copy(source, target, sems.at[count + number]))
    for copy in copies:
        copy.start()
    chips = places // 2
    for twin, ref in enumerate((own_ref, twin_ref)):
        part = ref[...].astype(jnp.float32)
        part = jnp.where(core == 1, pltpu.roll(part, part.shape[1] // 2, 1), part).astype(jnp.bfloat16)
        for number in range(chips):
            row = ((chip ^ turned(number, chips)) * 2 + (core + twin) % 2) * tokens
            here = pl.ds(pl.multiple_of(row, tokens), tokens)
            t_ref[here, :] = part[number * tokens : (number + 1) * tokens]
    for copy in copies:
        copy.wait()
    leave = pltpu.make_async_copy(x_ref, x_hbm, sems.at[0])
    leave.start()
    pass_on = pltpu.make_async_copy(sq_ref, sq_hbm, sems.at[1])
    for index in range(rows // block):
        here = rows_in(index, block)
        sq_ref[here, :] = dot(x_ref[here, :], wq_ref[...], 1, 1).astype(jnp.bfloat16)
        sk_ref[here, :] = dot(x_ref[here, :], wk_ref[...], 1, 1).astype(jnp.bfloat16)
    pass_on.start()
    gradients(
        t_ref, sk_ref, et_ref, es_ref, g_ref, heads=heads, chosen=range(heads), teach=teach, block=block
    )
    weight_grad(g_ref, x_ref, o_ref, 0, wk_ref.shape[0] // heads)
    leave.wait()
    pass_on.wait()


def query_kernel(
    x_hbm, s_hbm, t_ref, o_ref, x_ref, s_ref, et_ref, es_ref, g_ref, sems, *, heads, chosen, block
):
    first = pltpu.make_async_copy(s_hbm, s_ref, sems.at[0])
    fetch = pltpu.make_async_copy(x_hbm, x_ref, sems.at[1])
    first.start()
    fetch.start()
    first.wait()
    stud = s_ref.shape[1] // heads
    gradients(
        t_ref,
        s_ref,
        et_ref,
        es_ref,
        g_ref,
        heads=heads,
        chosen=chosen,
        teach=t_ref.shape[1] // heads,
        block=block,
    )
    fetch.wait()
    weight_grad(g_ref, x_ref, o_ref, chosen[0] * stud, stud)


def cost(rows, heads):
    return pl.CostEstimate(
        flops=2 * rows * rows * 256 * 3 * heads,
        bytes_accessed=4 * rows * rows,
        transcendentals=2 * rows * rows * heads,
    )


VMEM = pl.BlockSpec(memory_space=pltpu.VMEM)
HBM = pl.BlockSpec(memory_space=pltpu.HBM)
LIMIT = pltpu.CompilerParams(vmem_limit_bytes=20 * 2**20)


def in_hbm(*values):
    return [pltpu.with_memory_space_constraint(value, pltpu.HBM) for value in values]


def key_part(pieces, spots, w_query, w_key, own, twin, heads):
    feats, width = w_key.shape
    rows = 2 * own.shape[0]
    score = pltpu.VMEM((rows, rows), jnp.float32)
    return pl.pallas_call(
        functools.partial(
            key_kernel,
            spots=tuple(spots),
            heads=heads,
            teach=own.shape[1] // 2 // heads,
            block=math.gcd(rows, 256),
        ),
        out_shape=(
            pltpu.HBM((rows, width), jnp.bfloat16),
            pltpu.HBM((rows, feats), jnp.bfloat16),
            jax.ShapeDtypeStruct((feats, width), jnp.bfloat16),
        ),
        in_specs=[HBM] * (len(pieces) + 2) + [VMEM] * 2,
        out_specs=(HBM, HBM, VMEM),
        scratch_shapes=[
            pltpu.VMEM((rows, width), jnp.bfloat16),
            pltpu.VMEM((rows, feats), jnp.bfloat16),
            pltpu.VMEM(w_query.shape, jnp.bfloat16),
            pltpu.VMEM(w_key.shape, jnp.bfloat16),
            pltpu.VMEM((rows, feats), jnp.bfloat16),
            pltpu.VMEM((rows, own.shape[1]), jnp.bfloat16),
            score,
            score,
            pltpu.VMEM((rows, feats), jnp.float32),
            pltpu.SemaphoreType.DMA((len(pieces) + 2,)),
        ],
        compiler_params=LIMIT,
        cost_estimate=cost(rows, heads),
        name="key_type",
    )(*in_hbm(*pieces, w_query, w_key), own, twin)


def query_part(x, s, t, heads, chosen):
    rows, width = x.shape
    stud = s.shape[1] // heads
    score = pltpu.VMEM((rows, rows), jnp.float32)
    return pl.pallas_call(
        functools.partial(query_kernel, heads=heads, chosen=chosen, block=math.gcd(rows, 256)),
        out_shape=jax.ShapeDtypeStruct((len(chosen) * stud, width), jnp.bfloat16),
        in_specs=[HBM, HBM, VMEM],
        out_specs=VMEM,
        scratch_shapes=[
            pltpu.VMEM(x.shape, jnp.bfloat16),
            pltpu.VMEM(s.shape, jnp.bfloat16),
            score,
            score,
            pltpu.VMEM(s.shape, jnp.float32),
            pltpu.SemaphoreType.DMA((2,)),
        ],
        compiler_params=LIMIT,
        cost_estimate=cost(rows, len(chosen)),
        name="query_type",
    )(*in_hbm(x, s), t)


def by_sequence(teacher_q, teacher_k, student_in, w_query, w_key):
    places = lax.axis_size("ctx")
    levels = places // 4
    heads = HEADS // places
    index = lax.axis_index("head")
    own_k, own_x = (lax.dynamic_index_in_dim(value, index, 0, False) for value in (teacher_k, student_in))
    tokens = own_x.shape[0]

    ring = [2 * k for k in range(levels)] + [2 * k + 1 for k in reversed(range(levels))]
    count = len(ring)
    forward, backward, twin = [], [], []
    for position in range(count):
        for core in range(2):
            here = ring[position] * 2 + core
            forward.append((here, ring[(position + 1) % count] * 2 + core))
            backward.append((here, ring[position - 1] * 2 + core))
            twin.append((here, here ^ 1))

    pieces, spots = [], []

    def keep(value, step, offset=0):
        pieces.extend((value, lax.ppermute(value, "ctx", twin)))
        spots.extend(((step, 0, offset), (step, 1, offset)))

    chip = lax.axis_index("ctx") // 2
    keys = own_k
    bit = count // 2
    while bit:
        width = keys.shape[1] // 2
        mine = jnp.where(chip & bit, width, 0)
        stay = lax.dynamic_slice_in_dim(keys, mine, width, 1)
        leave = lax.dynamic_slice_in_dim(keys, width - mine, width, 1)
        got = lax.ppermute(leave, "ctx", [(i, i ^ (2 * bit)) for i in range(places)])
        keys = jnp.concatenate([stay, got])
        bit //= 2
    parts = split(teacher_q, places)
    half = tokens // 2
    keep(own_x, 0)
    ahead = behind = own_x
    for step in range(1, count // 2):
        ahead = lax.ppermute(ahead, "ctx", forward)
        behind = lax.ppermute(behind, "ctx", backward)
        keep(ahead, -step)
        keep(behind, step)
    ahead, behind, keys = lax.optimization_barrier((ahead, behind, keys))
    ahead = lax.ppermute(ahead[:half], "ctx", forward)
    behind = lax.ppermute(behind[half:], "ctx", backward)
    twin_keys = lax.ppermute(keys, "ctx", twin)
    keep(ahead, -(count // 2))
    keep(behind, count // 2, half)
    parts, _ = lax.optimization_barrier((parts, (ahead, behind)))
    tq = lax.all_to_all(parts, "ctx", 0, 0, tiled=True).reshape(places * tokens, parts.shape[2])

    x, s, part_k = key_part(pieces, spots, w_query, w_key, keys, twin_keys, heads)

    def swap(part):
        return lax.ppermute(part, "head", [(0, 1), (1, 0)])

    def both(part, other):
        return part.astype(jnp.float32) + other.astype(jnp.float32)

    groups = [tuple(range(lo, lo + heads // 2)) for lo in (0, heads // 2)]
    other_k = swap(part_k)
    parts = [query_part(x, s, tq, heads, chosen) for chosen in groups]
    others = [swap(part) for part in parts]
    other_k, parts[-1] = lax.optimization_barrier((other_k, parts[-1]))
    grad_q = jnp.concatenate([both(part, other) for part, other in zip(parts, others)])
    return grad_q, both(part_k, other_k)


def score_tile(local_part, key_part, offset, tile_width, head_width):
    key_tile = lax.dynamic_slice_in_dim(key_part, offset, tile_width, 2)
    product = lax.dot_general(
        local_part, key_tile, (((1,), (1,)), ((0,), (0,))), preferred_element_type=jnp.float32
    )
    return product / math.sqrt(head_width)


def by_rows(teacher_q, teacher_k, student_in, w_query, w_key):
    query_width = DTQ // HEADS
    key_width = DTK // HEADS
    stud_width = DS // HEADS
    batch_count = teacher_q.shape[0]
    share = teacher_q.shape[1] // lax.axis_size("head")
    first = lax.axis_index("head") * share
    own_query = lax.dynamic_slice_in_dim(teacher_q, first, share, 1)
    own_key = lax.dynamic_slice_in_dim(teacher_k, first, share, 1)
    own_input = lax.dynamic_slice_in_dim(student_in, first, share, 1)
    teach_query, teach_key = (
        lax.all_to_all(
            own_query.transpose(2, 0, 1), "ctx", split_axis=0, concat_axis=2, tiled=True
        ),
        lax.all_to_all(own_key.transpose(2, 0, 1), "ctx", split_axis=0, concat_axis=2, tiled=True),
    )
    student_rows = lax.all_gather(own_input, "ctx", axis=1, tiled=True)
    row_count = student_rows.shape[1]
    across = (((1,), (2,)), ((), ()))
    stud_query = lax.dot_general(
        w_query, student_rows, across, preferred_element_type=jnp.float32
    ).astype(jnp.bfloat16)
    stud_key = lax.dot_general(
        w_key, student_rows, across, preferred_element_type=jnp.float32
    ).astype(jnp.bfloat16)
    heads_here = stud_query.shape[0] // stud_width
    gathered_all = (
        lax.all_gather(teach_query, "head", axis=2, tiled=True),
        lax.all_gather(teach_key, "head", axis=2, tiled=True),
        lax.all_gather(stud_query, "head", axis=2, tiled=True),
        lax.all_gather(stud_key, "head", axis=2, tiled=True),
    )
    own_all = (teach_query, teach_key, stud_query, stud_key)
    key_count = gathered_all[0].shape[2]
    widths = (query_width, key_width, stud_width, stud_width)
    tile_width = math.gcd(key_count, 512)
    tile_count = key_count // tile_width
    tiles = jnp.arange(tile_count)
    batched = (((2,), (2,)), ((0,), (0,)))
    weight_query = jnp.zeros((heads_here * stud_width, w_query.shape[1]), jnp.float32)
    weight_key = jnp.zeros((heads_here * stud_width, w_key.shape[1]), jnp.float32)
    for index in range(batch_count):
        local_parts = tuple(
            (
                own_all[member][:, index, :].reshape(heads_here, widths[member], row_count)
                for member in range(4)
            )
        )
        key_parts = tuple(
            (
                gathered_all[member][:, index, :].reshape(heads_here, widths[member], key_count)
                for member in range(4)
            )
        )

        def stat_step(state_now, tile_index):
            offset = tile_index * tile_width
            updated = []
            for member in range(4):
                running_max, running_sum = state_now[member]
                scores = score_tile(
                    local_parts[member], key_parts[member], offset, tile_width, widths[member]
                )
                new_max = jnp.maximum(running_max, jnp.max(scores, axis=2))
                running_sum = running_sum * jnp.exp(running_max - new_max) + jnp.sum(
                    jnp.exp(scores - new_max[:, :, None]), axis=2
                )
                updated.append((new_max, running_sum))
            return (tuple(updated), None)

        start_stats = tuple(
            (
                (
                    jnp.full((heads_here, row_count), -jnp.inf, jnp.float32),
                    jnp.zeros((heads_here, row_count), jnp.float32),
                )
                for member in range(4)
            )
        )
        final_stats, unused = lax.scan(stat_step, start_stats, tiles)
        log_totals = tuple(
            (final_stats[member][0] + jnp.log(final_stats[member][1]) for member in range(4))
        )
        zero_terms = jnp.zeros((heads_here, stud_width, row_count), jnp.float32)

        def grad_step(state_now, tile_index):
            offset = tile_index * tile_width
            scores = [
                score_tile(
                    local_parts[member], key_parts[member], offset, tile_width, widths[member]
                )
                for member in range(4)
            ]
            row_probs = [
                jnp.exp(scores[member] - log_totals[member][:, :, None]) for member in range(4)
            ]
            differences = (
                (row_probs[2] - row_probs[0]).astype(jnp.bfloat16),
                (row_probs[3] - row_probs[1]).astype(jnp.bfloat16),
            )
            key_tiles = (
                lax.dynamic_slice_in_dim(key_parts[2], offset, tile_width, 2),
                lax.dynamic_slice_in_dim(key_parts[3], offset, tile_width, 2),
            )
            row_terms = tuple(
                (
                    state_now[member]
                    + lax.dot_general(
                        key_tiles[member],
                        differences[member],
                        batched,
                        preferred_element_type=jnp.float32,
                    )
                    for member in range(2)
                )
            )
            contrib = tuple(
                (
                    lax.dot_general(
                        local_parts[2 + member],
                        differences[member],
                        (((2,), (1,)), ((0,), (0,))),
                        preferred_element_type=jnp.float32,
                    )
                    for member in range(2)
                )
            )
            return (row_terms, contrib)

        sums, pieces = lax.scan(grad_step, (zero_terms, zero_terms), tiles)
        row_query, row_key = sums
        spread = tuple(
            (
                pieces[member].transpose(1, 2, 0, 3).reshape(heads_here, stud_width, key_count)
                for member in range(2)
            )
        )
        col_query, col_key = (
            lax.psum_scatter(
                spread[0].astype(jnp.bfloat16), "head", scatter_dimension=2, tiled=True
            ).astype(jnp.float32),
            lax.psum_scatter(
                spread[1].astype(jnp.bfloat16), "head", scatter_dimension=2, tiled=True
            ).astype(jnp.float32),
        )
        query_grad = (
            ((row_query + col_query) / math.sqrt(stud_width))
            .astype(jnp.bfloat16)
            .reshape(heads_here * stud_width, row_count)
        )
        key_grad = (
            ((row_key + col_key) / math.sqrt(stud_width))
            .astype(jnp.bfloat16)
            .reshape(heads_here * stud_width, row_count)
        )
        weight_query = weight_query + lax.dot_general(
            query_grad,
            student_rows[index],
            (((1,), (0,)), ((), ())),
            preferred_element_type=jnp.float32,
        )
        weight_key = weight_key + lax.dot_general(
            key_grad,
            student_rows[index],
            (((1,), (0,)), ((), ())),
            preferred_element_type=jnp.float32,
        )
    grad_query, grad_key = (
        lax.psum(weight_query.astype(jnp.bfloat16), "head").astype(jnp.float32),
        lax.psum(weight_key.astype(jnp.bfloat16), "head").astype(jnp.float32),
    )
    return (grad_query, grad_key)


def solution(mesh):
    placed = (
        P(None, "ctx", None),
        P(None, "ctx", None),
        P(None, "ctx", None),
        P("ctx", None),
        P("ctx", None),
    )
    places = mesh.shape["ctx"]

    def on_device(*args):
        batch, tokens, _ = args[0].shape
        even = places in (4, 8, 16, 32) and tokens % 32 == 0
        if even and batch == mesh.shape["head"] == 2 and tokens * places <= 1024:
            return by_sequence(*args)
        return by_rows(*args)

    return jax.shard_map(
        on_device,
        mesh=mesh,
        in_specs=placed,
        out_specs=(P("ctx", None), P("ctx", None)),
        check_vma=False,
    )
```

```python
import functools
import math

import jax
import jax.numpy as jnp
from jax import lax
from jax.experimental import pallas as pl
from jax.experimental.pallas import tpu as pltpu
from jax.sharding import PartitionSpec as P

DTQ = 8192
DTK = 1024
DS = 2048
HEADS = 64
LOG2E = 1.4426950408889634
SPREAD = 80.0


def dot(a, b, ca, cb):
    return lax.dot_general(a, b, (((ca,), (cb,)), ((), ())), preferred_element_type=jnp.float32)


def turned(number, count):
    return sum(((number >> bit) & 1) * (count >> (bit + 1)) for bit in range(count.bit_length() - 1))


def rows_in(index, block):
    return pl.ds(index * block, block)


def masked(value, head, width):
    lane = lax.broadcasted_iota(jnp.int32, value.shape, 1)
    keep = (lane >= head * width) & (lane < (head + 1) * width)
    return jnp.where(keep, value, jnp.zeros_like(value))


def norms(ref, width, chosen):
    first, last = chosen[0], chosen[-1] + 1
    if (first * width) % 128 == 0 and (last * width) % 128 == 0:
        value = ref[:, first * width : last * width].astype(jnp.float32)
    else:
        value, first = ref[...].astype(jnp.float32), 0
    square = (value * value).astype(jnp.bfloat16)
    column = lax.broadcasted_iota(jnp.int32, (square.shape[1], 128), 0) + first * width
    lane = lax.broadcasted_iota(jnp.int32, (square.shape[1], 128), 1)
    member = ((column >= lane * width) & (column < (lane + 1) * width)).astype(jnp.bfloat16)
    total = dot(square, member, 1, 0)
    factor = LOG2E / math.sqrt(width)
    high = jnp.max(total, axis=0, keepdims=True) * (factor * (1 + 2**-6))
    low = jnp.min(total, axis=0, keepdims=True) * (factor * (1 - 2**-6))
    lane = lax.broadcasted_iota(jnp.int32, (1, 128), 1)
    gap = jnp.where((lane >= chosen[0]) & (lane < last), high - low, 0.0)
    return high, jnp.max(gap)


def gradients(t_ref, s_ref, et_ref, es_ref, g_ref, gt_ref, *, heads, chosen, teach, block):
    rows, feats = s_ref.shape
    blocks = rows // block
    stud = feats // heads
    factors = tuple(LOG2E / math.sqrt(width) for width in (teach, stud))
    aligned = teach % 128 == 0

    def teacher(index, head):
        if aligned:
            part = t_ref.at[:, pl.ds(head * teach, teach)]
            return part[rows_in(index, block), :], part[...]
        return masked(t_ref[rows_in(index, block), :], head, teach), t_ref[...]

    def student(index, head):
        return masked(s_ref[rows_in(index, block), :], head, stud), s_ref[...]

    g_ref[...] = jnp.zeros_like(g_ref)
    gt_ref[...] = jnp.zeros_like(gt_ref)
    top_t, gap_t = norms(t_ref, teach, chosen)
    top_s, gap_s = norms(s_ref, stud, chosen)
    safe = jnp.maximum(gap_t, gap_s) < SPREAD

    @pl.when(safe)
    def _():
        flipped = s_ref[...].T
        for head in chosen:
            pick = slice(head, head + 1)
            sums = []
            for own, e_ref, factor, top in (
                (teacher, et_ref, factors[0], top_t[:, pick]),
                (student, es_ref, factors[1], top_s[:, pick]),
            ):
                down = [jnp.zeros((1, block), jnp.float32) for _ in range(blocks)]
                along = []
                for index in range(blocks):
                    left, right = own(index, head)
                    lo = index * block
                    e = jnp.exp2(dot(left, right[lo:], 1, 1) * factor - top)
                    e_ref[rows_in(index, block), lo:] = e
                    for other in range(index, blocks):
                        part = e[:, other * block - lo : (other + 1) * block - lo]
                        down[other] = down[other] + jnp.sum(part, axis=0, keepdims=True)
                    width = math.gcd(block, 128)
                    parts = [e[:, at : at + width] for at in range(block, e.shape[1], width)]
                    along.append(sum(parts) if parts else jnp.zeros((block, width), jnp.float32))
                along = jnp.sum(jnp.concatenate(along, axis=0).T, axis=0, keepdims=True)
                sums.append(jnp.concatenate(down, axis=1) + along)
            across = [1.0 / total for total in sums]
            down = [jnp.broadcast_to(a, (128, rows)).T[:, :1] for a in across]
            right = masked(s_ref[...], head, stud)
            for index in range(blocks):
                lo = index * block
                here = rows_in(index, block)
                h = es_ref[here, lo:] * (down[1][lo : lo + block] + across[1][:, lo:])
                h = h - et_ref[here, lo:] * (down[0][lo : lo + block] + across[0][:, lo:])
                h = h.astype(jnp.bfloat16)
                g_ref[here, :] += dot(h, right[lo:], 1, 0)
                if index < blocks - 1:
                    feats_here = slice(head * stud, (head + 1) * stud)
                    left = flipped[feats_here, lo : lo + block]
                    gt_ref[feats_here, lo + block :] += dot(left, h[:, block:], 1, 0)

    @pl.when(jnp.logical_not(safe))
    def _():
        for head in chosen:

            def step(index, carry):
                here = rows_in(index, block)
                probs = []
                for k, own in enumerate((teacher, student)):
                    left, right = own(index, head)
                    score = dot(left, right, 1, 1) * (factors[k] / LOG2E)
                    e = jnp.exp(score - jnp.max(score, axis=1, keepdims=True))
                    probs.append(e / jnp.sum(e, axis=1, keepdims=True))
                difference = probs[1] - probs[0]
                right = masked(s_ref[...], head, stud)
                g_ref[here, :] += dot(difference.astype(jnp.bfloat16), right, 1, 0)
                left = masked(s_ref[here, :], head, stud)
                g_ref[...] += dot(difference.T.astype(jnp.bfloat16), left, 1, 0)
                return carry

            lax.fori_loop(0, blocks, step, 0)


def weight_grad(g_ref, gt_ref, x_ref, o_ref, first, stud):
    grad = ((g_ref[...].T + gt_ref[...]) * (1.0 / math.sqrt(stud))).astype(jnp.bfloat16)
    grad = grad[first : first + o_ref.shape[0]]
    columns = math.gcd(x_ref.shape[1], 512)
    for lo in range(0, x_ref.shape[1], columns):
        part = pl.ds(lo, columns)
        o_ref[:, part] = dot(grad, x_ref[:, part], 1, 0).astype(jnp.bfloat16)


def split_kernel(t_ref, o_ref, sems):
    own = t_ref.at[lax.axis_index("head")]
    places, _, width = o_ref.shape
    copies = [
        pltpu.make_async_copy(own.at[:, pl.ds(place * width, width)], o_ref.at[place], sems.at[place])
        for place in range(places)
    ]
    for copy in copies:
        copy.start()
    for copy in copies:
        copy.wait()


def split(t, places):
    return pl.pallas_call(
        split_kernel,
        out_shape=jax.ShapeDtypeStruct((places, t.shape[1], t.shape[2] // places), t.dtype),
        in_specs=[HBM],
        out_specs=VMEM,
        scratch_shapes=[pltpu.SemaphoreType.DMA((places,))],
        name="split",
    )(t)


def key_kernel(*refs, spots, heads, teach, block):
    count = len(spots)
    pieces, refs = refs[:count], refs[count:]
    wq_hbm, wk_hbm, own_ref, twin_ref, x_hbm, sq_ref, o_ref, *refs = refs
    x_ref, wq_ref, wk_ref, sk_ref, t_ref, et_ref, es_ref, g_ref, gt_ref, sems = refs
    places = lax.axis_size("ctx")
    where = lax.axis_index("ctx")
    levels = places // 4
    rows = x_ref.shape[0]
    tokens = rows // places
    chip, core = where // 2, where % 2
    level, side = chip // 2, chip % 2
    position = jnp.where(side == 0, level, 2 * levels - 1 - level)
    copies = []
    for number, (piece, (step, twin, offset)) in enumerate(zip(pieces, spots)):
        other = (position + step + 2 * levels) % (2 * levels)
        other = jnp.where(other < levels, 2 * other, 2 * (2 * levels - 1 - other) + 1)
        row = pl.multiple_of((other * 2 + (core + twin) % 2) * tokens + offset, piece.shape[0])
        target = x_ref.at[pl.ds(row, piece.shape[0]), :]
        copies.append(pltpu.make_async_copy(piece, target, sems.at[number]))
    for number, (source, target) in enumerate(((wq_hbm, wq_ref), (wk_hbm, wk_ref))):
        copies.append(pltpu.make_async_copy(source, target, sems.at[count + number]))
    for copy in copies:
        copy.start()
    chips = places // 2
    for twin, ref in enumerate((own_ref, twin_ref)):
        part = ref[...].astype(jnp.float32)
        part = jnp.where(core == 1, pltpu.roll(part, part.shape[1] // 2, 1), part).astype(jnp.bfloat16)
        for number in range(chips):
            row = ((chip ^ turned(number, chips)) * 2 + (core + twin) % 2) * tokens
            here = pl.ds(pl.multiple_of(row, tokens), tokens)
            t_ref[here, :] = part[number * tokens : (number + 1) * tokens]
    for copy in copies:
        copy.wait()
    leave = pltpu.make_async_copy(x_ref, x_hbm, sems.at[0])
    leave.start()
    for index in range(rows // block):
        here = rows_in(index, block)
        sq_ref[here, :] = dot(x_ref[here, :], wq_ref[...], 1, 1).astype(jnp.bfloat16)
        sk_ref[here, :] = dot(x_ref[here, :], wk_ref[...], 1, 1).astype(jnp.bfloat16)
    gradients(
        t_ref,
        sk_ref,
        et_ref,
        es_ref,
        g_ref,
        gt_ref,
        heads=heads,
        chosen=range(heads),
        teach=teach,
        block=block,
    )
    weight_grad(g_ref, gt_ref, x_ref, o_ref, 0, wk_ref.shape[0] // heads)
    leave.wait()


def query_kernel(
    x_hbm, s_ref, t_ref, o_ref, x_ref, et_ref, es_ref, g_ref, gt_ref, sem, *, heads, chosen, block
):
    fetch = pltpu.make_async_copy(x_hbm, x_ref, sem)
    fetch.start()
    stud = s_ref.shape[1] // heads
    gradients(
        t_ref,
        s_ref,
        et_ref,
        es_ref,
        g_ref,
        gt_ref,
        heads=heads,
        chosen=chosen,
        teach=t_ref.shape[1] // heads,
        block=block,
    )
    fetch.wait()
    weight_grad(g_ref, gt_ref, x_ref, o_ref, chosen[0] * stud, stud)


def cost(rows, heads):
    return pl.CostEstimate(
        flops=2 * rows * rows * 256 * 3 * heads,
        bytes_accessed=4 * rows * rows,
        transcendentals=2 * rows * rows * heads,
    )


VMEM = pl.BlockSpec(memory_space=pltpu.VMEM)
HBM = pl.BlockSpec(memory_space=pltpu.HBM)
LIMIT = pltpu.CompilerParams(vmem_limit_bytes=20 * 2**20)


def in_hbm(*values):
    return [pltpu.with_memory_space_constraint(value, pltpu.HBM) for value in values]


def key_part(pieces, spots, w_query, w_key, own, twin, heads):
    feats, width = w_key.shape
    rows = 2 * own.shape[0]
    score = pltpu.VMEM((rows, rows), jnp.float32)
    return pl.pallas_call(
        functools.partial(
            key_kernel,
            spots=tuple(spots),
            heads=heads,
            teach=own.shape[1] // 2 // heads,
            block=math.gcd(rows, 256),
        ),
        out_shape=(
            pltpu.HBM((rows, width), jnp.bfloat16),
            pltpu.VMEM((rows, feats), jnp.bfloat16),
            jax.ShapeDtypeStruct((feats, width), jnp.bfloat16),
        ),
        in_specs=[HBM] * (len(pieces) + 2) + [VMEM] * 2,
        out_specs=(HBM, VMEM, VMEM),
        scratch_shapes=[
            pltpu.VMEM((rows, width), jnp.bfloat16),
            pltpu.VMEM(w_query.shape, jnp.bfloat16),
            pltpu.VMEM(w_key.shape, jnp.bfloat16),
            pltpu.VMEM((rows, feats), jnp.bfloat16),
            pltpu.VMEM((rows, own.shape[1]), jnp.bfloat16),
            score,
            score,
            pltpu.VMEM((rows, feats), jnp.float32),
            pltpu.VMEM((feats, rows), jnp.float32),
            pltpu.SemaphoreType.DMA((len(pieces) + 2,)),
        ],
        compiler_params=LIMIT,
        cost_estimate=cost(rows, heads),
        name="key_type",
    )(*in_hbm(*pieces, w_query, w_key), own, twin)


def query_part(x, s, t, heads, chosen):
    rows, width = x.shape
    stud = s.shape[1] // heads
    score = pltpu.VMEM((rows, rows), jnp.float32)
    return pl.pallas_call(
        functools.partial(query_kernel, heads=heads, chosen=chosen, block=math.gcd(rows, 256)),
        out_shape=jax.ShapeDtypeStruct((len(chosen) * stud, width), jnp.bfloat16),
        in_specs=[HBM, VMEM, VMEM],
        out_specs=VMEM,
        scratch_shapes=[
            pltpu.VMEM(x.shape, jnp.bfloat16),
            score,
            score,
            pltpu.VMEM(s.shape, jnp.float32),
            pltpu.VMEM(s.shape[::-1], jnp.float32),
            pltpu.SemaphoreType.DMA,
        ],
        compiler_params=LIMIT,
        cost_estimate=cost(rows, len(chosen)),
        name="query_type",
    )(*in_hbm(x), pltpu.with_memory_space_constraint(s, pltpu.VMEM), t)


def by_sequence(teacher_q, teacher_k, student_in, w_query, w_key):
    places = lax.axis_size("ctx")
    levels = places // 4
    heads = HEADS // places
    index = lax.axis_index("head")
    own_k, own_x = (lax.dynamic_index_in_dim(value, index, 0, False) for value in (teacher_k, student_in))
    tokens = own_x.shape[0]

    ring = [2 * k for k in range(levels)] + [2 * k + 1 for k in reversed(range(levels))]
    count = len(ring)
    forward, backward, twin = [], [], []
    for position in range(count):
        for core in range(2):
            here = ring[position] * 2 + core
            forward.append((here, ring[(position + 1) % count] * 2 + core))
            backward.append((here, ring[position - 1] * 2 + core))
            twin.append((here, here ^ 1))

    pieces, spots = [], []

    def keep(value, step, offset=0):
        pieces.extend((value, lax.ppermute(value, "ctx", twin)))
        spots.extend(((step, 0, offset), (step, 1, offset)))

    chip = lax.axis_index("ctx") // 2

    def halve(keys, bit):
        width = keys.shape[1] // 2
        mine = jnp.where(chip & bit, width, 0)
        stay = lax.dynamic_slice_in_dim(keys, mine, width, 1)
        leave = lax.dynamic_slice_in_dim(keys, width - mine, width, 1)
        got = lax.ppermute(leave, "ctx", [(i, i ^ (2 * bit)) for i in range(places)])
        return stay, got

    half = tokens // 2
    bits = [1 << bit for bit in reversed(range(count.bit_length() - 1))]
    pair = halve(own_k, bits.pop(0))
    parts = split(teacher_q, places)
    keep(own_x, 0)
    ahead = behind = own_x
    for step in range(1, count // 2):
        ahead = lax.ppermute(ahead, "ctx", forward)
        behind = lax.ppermute(behind, "ctx", backward)
        keep(ahead, -step)
        keep(behind, step)
        if bits:
            ahead, behind, pair = lax.optimization_barrier((ahead, behind, pair))
            pair = halve(jnp.concatenate(pair), bits.pop(0))
    ahead = lax.ppermute(ahead[:half], "ctx", forward)
    behind = lax.ppermute(behind[half:], "ctx", backward)
    keep(ahead, -(count // 2))
    keep(behind, count // 2, half)
    for bit in bits:
        pair = halve(jnp.concatenate(pair), bit)
    keys = jnp.concatenate(pair)
    twin_keys = lax.ppermute(keys, "ctx", twin)

    parts, _, keys = lax.optimization_barrier((parts, (ahead, behind), keys))
    tq = lax.all_to_all(parts, "ctx", 0, 0, tiled=True).reshape(places * tokens, parts.shape[2])

    x, s, part_k = key_part(pieces, spots, w_query, w_key, keys, twin_keys, heads)

    def swap(part):
        return lax.ppermute(part, "head", [(0, 1), (1, 0)])

    def both(part, other):
        return part.astype(jnp.float32) + other.astype(jnp.float32)

    first, last = (tuple(range(lo, lo + heads // 2)) for lo in (0, heads // 2))
    other_k = swap(part_k)
    part = query_part(x, s, tq, heads, first)
    other = swap(part)
    s, part = lax.optimization_barrier((s, part))
    part_last = query_part(x, s, tq, heads, last)
    other_last = swap(part_last)
    other_k, other, part_last = lax.optimization_barrier((other_k, other, part_last))
    grad_q = jnp.pad(both(part, other), ((0, part_last.shape[0]), (0, 0)))
    grad_q = lax.dynamic_update_slice(grad_q, both(part_last, other_last), (part.shape[0], 0))
    return grad_q, both(part_k, other_k)


def score_tile(local_part, key_part, offset, tile_width, head_width):
    key_tile = lax.dynamic_slice_in_dim(key_part, offset, tile_width, 2)
    product = lax.dot_general(
        local_part, key_tile, (((1,), (1,)), ((0,), (0,))), preferred_element_type=jnp.float32
    )
    return product / math.sqrt(head_width)


def by_rows(teacher_q, teacher_k, student_in, w_query, w_key):
    query_width = DTQ // HEADS
    key_width = DTK // HEADS
    stud_width = DS // HEADS
    batch_count = teacher_q.shape[0]
    share = teacher_q.shape[1] // lax.axis_size("head")
    first = lax.axis_index("head") * share
    own_query = lax.dynamic_slice_in_dim(teacher_q, first, share, 1)
    own_key = lax.dynamic_slice_in_dim(teacher_k, first, share, 1)
    own_input = lax.dynamic_slice_in_dim(student_in, first, share, 1)
    teach_query, teach_key = (
        lax.all_to_all(
            own_query.transpose(2, 0, 1), "ctx", split_axis=0, concat_axis=2, tiled=True
        ),
        lax.all_to_all(own_key.transpose(2, 0, 1), "ctx", split_axis=0, concat_axis=2, tiled=True),
    )
    student_rows = lax.all_gather(own_input, "ctx", axis=1, tiled=True)
    row_count = student_rows.shape[1]
    across = (((1,), (2,)), ((), ()))
    stud_query = lax.dot_general(
        w_query, student_rows, across, preferred_element_type=jnp.float32
    ).astype(jnp.bfloat16)
    stud_key = lax.dot_general(
        w_key, student_rows, across, preferred_element_type=jnp.float32
    ).astype(jnp.bfloat16)
    heads_here = stud_query.shape[0] // stud_width
    gathered_all = (
        lax.all_gather(teach_query, "head", axis=2, tiled=True),
        lax.all_gather(teach_key, "head", axis=2, tiled=True),
        lax.all_gather(stud_query, "head", axis=2, tiled=True),
        lax.all_gather(stud_key, "head", axis=2, tiled=True),
    )
    own_all = (teach_query, teach_key, stud_query, stud_key)
    key_count = gathered_all[0].shape[2]
    widths = (query_width, key_width, stud_width, stud_width)
    tile_width = math.gcd(key_count, 512)
    tile_count = key_count // tile_width
    tiles = jnp.arange(tile_count)
    batched = (((2,), (2,)), ((0,), (0,)))
    weight_query = jnp.zeros((heads_here * stud_width, w_query.shape[1]), jnp.float32)
    weight_key = jnp.zeros((heads_here * stud_width, w_key.shape[1]), jnp.float32)
    for index in range(batch_count):
        local_parts = tuple(
            (
                own_all[member][:, index, :].reshape(heads_here, widths[member], row_count)
                for member in range(4)
            )
        )
        key_parts = tuple(
            (
                gathered_all[member][:, index, :].reshape(heads_here, widths[member], key_count)
                for member in range(4)
            )
        )

        def stat_step(state_now, tile_index):
            offset = tile_index * tile_width
            updated = []
            for member in range(4):
                running_max, running_sum = state_now[member]
                scores = score_tile(
                    local_parts[member], key_parts[member], offset, tile_width, widths[member]
                )
                new_max = jnp.maximum(running_max, jnp.max(scores, axis=2))
                running_sum = running_sum * jnp.exp(running_max - new_max) + jnp.sum(
                    jnp.exp(scores - new_max[:, :, None]), axis=2
                )
                updated.append((new_max, running_sum))
            return (tuple(updated), None)

        start_stats = tuple(
            (
                (
                    jnp.full((heads_here, row_count), -jnp.inf, jnp.float32),
                    jnp.zeros((heads_here, row_count), jnp.float32),
                )
                for member in range(4)
            )
        )
        final_stats, unused = lax.scan(stat_step, start_stats, tiles)
        log_totals = tuple(
            (final_stats[member][0] + jnp.log(final_stats[member][1]) for member in range(4))
        )
        zero_terms = jnp.zeros((heads_here, stud_width, row_count), jnp.float32)

        def grad_step(state_now, tile_index):
            offset = tile_index * tile_width
            scores = [
                score_tile(
                    local_parts[member], key_parts[member], offset, tile_width, widths[member]
                )
                for member in range(4)
            ]
            row_probs = [
                jnp.exp(scores[member] - log_totals[member][:, :, None]) for member in range(4)
            ]
            differences = (
                (row_probs[2] - row_probs[0]).astype(jnp.bfloat16),
                (row_probs[3] - row_probs[1]).astype(jnp.bfloat16),
            )
            key_tiles = (
                lax.dynamic_slice_in_dim(key_parts[2], offset, tile_width, 2),
                lax.dynamic_slice_in_dim(key_parts[3], offset, tile_width, 2),
            )
            row_terms = tuple(
                (
                    state_now[member]
                    + lax.dot_general(
                        key_tiles[member],
                        differences[member],
                        batched,
                        preferred_element_type=jnp.float32,
                    )
                    for member in range(2)
                )
            )
            contrib = tuple(
                (
                    lax.dot_general(
                        local_parts[2 + member],
                        differences[member],
                        (((2,), (1,)), ((0,), (0,))),
                        preferred_element_type=jnp.float32,
                    )
                    for member in range(2)
                )
            )
            return (row_terms, contrib)

        sums, pieces = lax.scan(grad_step, (zero_terms, zero_terms), tiles)
        row_query, row_key = sums
        spread = tuple(
            (
                pieces[member].transpose(1, 2, 0, 3).reshape(heads_here, stud_width, key_count)
                for member in range(2)
            )
        )
        col_query, col_key = (
            lax.psum_scatter(
                spread[0].astype(jnp.bfloat16), "head", scatter_dimension=2, tiled=True
            ).astype(jnp.float32),
            lax.psum_scatter(
                spread[1].astype(jnp.bfloat16), "head", scatter_dimension=2, tiled=True
            ).astype(jnp.float32),
        )
        query_grad = (
            ((row_query + col_query) / math.sqrt(stud_width))
            .astype(jnp.bfloat16)
            .reshape(heads_here * stud_width, row_count)
        )
        key_grad = (
            ((row_key + col_key) / math.sqrt(stud_width))
            .astype(jnp.bfloat16)
            .reshape(heads_here * stud_width, row_count)
        )
        weight_query = weight_query + lax.dot_general(
            query_grad,
            student_rows[index],
            (((1,), (0,)), ((), ())),
            preferred_element_type=jnp.float32,
        )
        weight_key = weight_key + lax.dot_general(
            key_grad,
            student_rows[index],
            (((1,), (0,)), ((), ())),
            preferred_element_type=jnp.float32,
        )
    grad_query, grad_key = (
        lax.psum(weight_query.astype(jnp.bfloat16), "head").astype(jnp.float32),
        lax.psum(weight_key.astype(jnp.bfloat16), "head").astype(jnp.float32),
    )
    return (grad_query, grad_key)


def solution(mesh):
    placed = (
        P(None, "ctx", None),
        P(None, "ctx", None),
        P(None, "ctx", None),
        P("ctx", None),
        P("ctx", None),
    )
    places = mesh.shape["ctx"]

    def on_device(*args):
        batch, tokens, _ = args[0].shape
        even = places in (4, 8, 16, 32) and tokens % 32 == 0
        if even and batch == mesh.shape["head"] == 2 and tokens * places <= 1024:
            return by_sequence(*args)
        return by_rows(*args)

    return jax.shard_map(
        on_device,
        mesh=mesh,
        in_specs=placed,
        out_specs=(P("ctx", None), P("ctx", None)),
        check_vma=False,
    )
```

```python
import functools
import math

import jax
import jax.numpy as jnp
from jax import lax
from jax.experimental import pallas as pl
from jax.experimental.pallas import tpu as pltpu
from jax.sharding import PartitionSpec as P

DTQ = 8192
DTK = 1024
DS = 2048
HEADS = 64
LOG2E = 1.4426950408889634
SPREAD = 80.0


def dot(a, b, ca, cb):
    return lax.dot_general(a, b, (((ca,), (cb,)), ((), ())), preferred_element_type=jnp.float32)


def rows_in(index, block):
    return pl.ds(index * block, block)


def masked(value, head, width):
    lane = lax.broadcasted_iota(jnp.int32, value.shape, 1)
    keep = (lane >= head * width) & (lane < (head + 1) * width)
    return jnp.where(keep, value, jnp.zeros_like(value))


def norms(ref, width, chosen):
    first, last = chosen[0], chosen[-1] + 1
    if (first * width) % 128 == 0 and (last * width) % 128 == 0:
        value = ref[:, first * width : last * width].astype(jnp.float32)
    else:
        value, first = ref[...].astype(jnp.float32), 0
    square = (value * value).astype(jnp.bfloat16)
    column = lax.broadcasted_iota(jnp.int32, (square.shape[1], 128), 0) + first * width
    lane = lax.broadcasted_iota(jnp.int32, (square.shape[1], 128), 1)
    member = ((column >= lane * width) & (column < (lane + 1) * width)).astype(jnp.bfloat16)
    total = dot(square, member, 1, 0)
    factor = LOG2E / math.sqrt(width)
    high = jnp.max(total, axis=0, keepdims=True) * (factor * (1 + 2**-6))
    low = jnp.min(total, axis=0, keepdims=True) * (factor * (1 - 2**-6))
    lane = lax.broadcasted_iota(jnp.int32, (1, 128), 1)
    gap = jnp.where((lane >= chosen[0]) & (lane < last), high - low, 0.0)
    return high, jnp.max(gap)


def gradients(t_ref, s_ref, et_ref, es_ref, g_ref, gt_ref, *, heads, chosen, teach, block):
    rows, feats = s_ref.shape
    blocks = rows // block
    stud = feats // heads
    factors = tuple(LOG2E / math.sqrt(width) for width in (teach, stud))
    aligned = teach % 128 == 0

    def teacher(index, head):
        if aligned:
            part = t_ref.at[:, pl.ds(head * teach, teach)]
            return part[rows_in(index, block), :], part[...]
        return masked(t_ref[rows_in(index, block), :], head, teach), t_ref[...]

    def student(index, head):
        return masked(s_ref[rows_in(index, block), :], head, stud), s_ref[...]

    g_ref[...] = jnp.zeros_like(g_ref)
    gt_ref[...] = jnp.zeros_like(gt_ref)
    top_t, gap_t = norms(t_ref, teach, chosen)
    top_s, gap_s = norms(s_ref, stud, chosen)
    safe = jnp.maximum(gap_t, gap_s) < SPREAD

    @pl.when(safe)
    def _():
        flipped = s_ref[...].T
        for head in chosen:
            pick = slice(head, head + 1)
            sums = []
            for own, e_ref, factor, top in (
                (teacher, et_ref, factors[0], top_t[:, pick]),
                (student, es_ref, factors[1], top_s[:, pick]),
            ):
                down = [jnp.zeros((1, block), jnp.float32) for _ in range(blocks)]
                along = []
                for index in range(blocks):
                    left, right = own(index, head)
                    lo = index * block
                    e = jnp.exp2(dot(left, right[lo:], 1, 1) * factor - top)
                    e_ref[rows_in(index, block), lo:] = e
                    for other in range(index, blocks):
                        part = e[:, other * block - lo : (other + 1) * block - lo]
                        down[other] = down[other] + jnp.sum(part, axis=0, keepdims=True)
                    width = math.gcd(block, 128)
                    parts = [e[:, at : at + width] for at in range(block, e.shape[1], width)]
                    along.append(sum(parts) if parts else jnp.zeros((block, width), jnp.float32))
                along = jnp.sum(jnp.concatenate(along, axis=0).T, axis=0, keepdims=True)
                sums.append(jnp.concatenate(down, axis=1) + along)
            across = [1.0 / total for total in sums]
            down = [jnp.broadcast_to(a, (128, rows)).T[:, :1] for a in across]
            right = masked(s_ref[...], head, stud)
            for index in range(blocks):
                lo = index * block
                here = rows_in(index, block)
                h = es_ref[here, lo:] * (down[1][lo : lo + block] + across[1][:, lo:])
                h = h - et_ref[here, lo:] * (down[0][lo : lo + block] + across[0][:, lo:])
                h = h.astype(jnp.bfloat16)
                g_ref[here, :] += dot(h, right[lo:], 1, 0)
                if index < blocks - 1:
                    feats_here = slice(head * stud, (head + 1) * stud)
                    left = flipped[feats_here, lo : lo + block]
                    gt_ref[feats_here, lo + block :] += dot(left, h[:, block:], 1, 0)

    @pl.when(jnp.logical_not(safe))
    def _():
        for head in chosen:

            def step(index, carry):
                here = rows_in(index, block)
                probs = []
                for k, own in enumerate((teacher, student)):
                    left, right = own(index, head)
                    score = dot(left, right, 1, 1) * (factors[k] / LOG2E)
                    e = jnp.exp(score - jnp.max(score, axis=1, keepdims=True))
                    probs.append(e / jnp.sum(e, axis=1, keepdims=True))
                difference = probs[1] - probs[0]
                right = masked(s_ref[...], head, stud)
                g_ref[here, :] += dot(difference.astype(jnp.bfloat16), right, 1, 0)
                left = masked(s_ref[here, :], head, stud)
                g_ref[...] += dot(difference.T.astype(jnp.bfloat16), left, 1, 0)
                return carry

            lax.fori_loop(0, blocks, step, 0)


def weight_grad(g_ref, gt_ref, x_ref, o_ref, first, stud):
    grad = ((g_ref[...].T + gt_ref[...]) * (1.0 / math.sqrt(stud))).astype(jnp.bfloat16)
    grad = grad[first : first + o_ref.shape[0]]
    columns = math.gcd(x_ref.shape[1], 512)
    for lo in range(0, x_ref.shape[1], columns):
        part = pl.ds(lo, columns)
        o_ref[:, part] = dot(grad, x_ref[:, part], 1, 0).astype(jnp.bfloat16)


def split_kernel(t_ref, o_ref, sems):
    own = t_ref.at[lax.axis_index("head")]
    places, _, width = o_ref.shape
    copies = [
        pltpu.make_async_copy(own.at[:, pl.ds(place * width, width)], o_ref.at[place], sems.at[place])
        for place in range(places)
    ]
    for copy in copies:
        copy.start()
    for copy in copies:
        copy.wait()


def split(t, places):
    return pl.pallas_call(
        split_kernel,
        out_shape=jax.ShapeDtypeStruct((places, t.shape[1], t.shape[2] // places), t.dtype),
        in_specs=[HBM],
        out_specs=VMEM,
        scratch_shapes=[pltpu.SemaphoreType.DMA((places,))],
        name="split",
    )(t)


def key_kernel(*refs, spots, heads, teach, block):
    count = len(spots)
    pieces, refs = refs[:count], refs[count:]
    wq_hbm, wk_hbm, own_ref, twin_ref, x_hbm, sq_ref, o_ref, *refs = refs
    x_ref, wq_ref, wk_ref, sk_ref, t_ref, et_ref, es_ref, g_ref, gt_ref, sems = refs
    places = lax.axis_size("ctx")
    where = lax.axis_index("ctx")
    levels = places // 4
    rows = x_ref.shape[0]
    tokens = rows // places
    chip, core = where // 2, where % 2
    level, side = chip // 2, chip % 2
    position = jnp.where(side == 0, level, 2 * levels - 1 - level)
    copies = []
    for number, (piece, (step, twin, offset)) in enumerate(zip(pieces, spots)):
        other = (position + step + 2 * levels) % (2 * levels)
        other = jnp.where(other < levels, 2 * other, 2 * (2 * levels - 1 - other) + 1)
        row = pl.multiple_of((other * 2 + (core + twin) % 2) * tokens + offset, piece.shape[0])
        target = x_ref.at[pl.ds(row, piece.shape[0]), :]
        copies.append(pltpu.make_async_copy(piece, target, sems.at[number]))
    for number, (source, target) in enumerate(((wq_hbm, wq_ref), (wk_hbm, wk_ref))):
        copies.append(pltpu.make_async_copy(source, target, sems.at[count + number]))
    for copy in copies:
        copy.start()
    chips = places // 2
    for twin, ref in enumerate((own_ref, twin_ref)):
        part = ref[...].astype(jnp.float32)
        part = jnp.where(core == 1, pltpu.roll(part, part.shape[1] // 2, 1), part).astype(jnp.bfloat16)
        for number in range(chips):
            row = ((chip ^ (2 * (number % levels) + number // levels)) * 2 + (core + twin) % 2) * tokens
            here = pl.ds(pl.multiple_of(row, tokens), tokens)
            t_ref[here, :] = part[number * tokens : (number + 1) * tokens]
    for copy in copies:
        copy.wait()
    leave = pltpu.make_async_copy(x_ref, x_hbm, sems.at[0])
    leave.start()
    for index in range(rows // block):
        here = rows_in(index, block)
        sq_ref[here, :] = dot(x_ref[here, :], wq_ref[...], 1, 1).astype(jnp.bfloat16)
        sk_ref[here, :] = dot(x_ref[here, :], wk_ref[...], 1, 1).astype(jnp.bfloat16)
    gradients(
        t_ref,
        sk_ref,
        et_ref,
        es_ref,
        g_ref,
        gt_ref,
        heads=heads,
        chosen=range(heads),
        teach=teach,
        block=block,
    )
    weight_grad(g_ref, gt_ref, x_ref, o_ref, 0, wk_ref.shape[0] // heads)
    leave.wait()


def query_kernel(
    x_hbm, s_ref, t_ref, o_ref, x_ref, et_ref, es_ref, g_ref, gt_ref, sem, *, heads, chosen, block
):
    fetch = pltpu.make_async_copy(x_hbm, x_ref, sem)
    fetch.start()
    stud = s_ref.shape[1] // heads
    gradients(
        t_ref,
        s_ref,
        et_ref,
        es_ref,
        g_ref,
        gt_ref,
        heads=heads,
        chosen=chosen,
        teach=t_ref.shape[1] // heads,
        block=block,
    )
    fetch.wait()
    weight_grad(g_ref, gt_ref, x_ref, o_ref, chosen[0] * stud, stud)


def cost(rows, heads):
    return pl.CostEstimate(
        flops=2 * rows * rows * 256 * 3 * heads,
        bytes_accessed=4 * rows * rows,
        transcendentals=2 * rows * rows * heads,
    )


VMEM = pl.BlockSpec(memory_space=pltpu.VMEM)
HBM = pl.BlockSpec(memory_space=pltpu.HBM)
LIMIT = pltpu.CompilerParams(vmem_limit_bytes=20 * 2**20)


def in_hbm(*values):
    return [pltpu.with_memory_space_constraint(value, pltpu.HBM) for value in values]


def in_vmem(*values):
    return [pltpu.with_memory_space_constraint(value, pltpu.VMEM) for value in values]


def key_part(pieces, spots, w_query, w_key, own, twin, heads):
    feats, width = w_key.shape
    rows = 2 * own.shape[0]
    score = pltpu.VMEM((rows, rows), jnp.float32)
    late = [put(value) for put, value in zip((in_hbm, in_vmem) * 2 + (in_vmem,) * 4, pieces[-8:])]
    late = [value for (value,) in late]
    kept = [HBM] * (len(pieces) - 8) + [HBM, VMEM] * 2 + [VMEM] * 4
    return pl.pallas_call(
        functools.partial(
            key_kernel,
            spots=tuple(spots),
            heads=heads,
            teach=own.shape[1] // 2 // heads,
            block=math.gcd(rows, 256),
        ),
        out_shape=(
            pltpu.HBM((rows, width), jnp.bfloat16),
            pltpu.VMEM((rows, feats), jnp.bfloat16),
            jax.ShapeDtypeStruct((feats, width), jnp.bfloat16),
        ),
        in_specs=kept + [HBM] * 2 + [VMEM] * 2,
        out_specs=(HBM, VMEM, VMEM),
        scratch_shapes=[
            pltpu.VMEM((rows, width), jnp.bfloat16),
            pltpu.VMEM(w_query.shape, jnp.bfloat16),
            pltpu.VMEM(w_key.shape, jnp.bfloat16),
            pltpu.VMEM((rows, feats), jnp.bfloat16),
            pltpu.VMEM((rows, own.shape[1]), jnp.bfloat16),
            score,
            score,
            pltpu.VMEM((rows, feats), jnp.float32),
            pltpu.VMEM((feats, rows), jnp.float32),
            pltpu.SemaphoreType.DMA((len(pieces) + 2,)),
        ],
        compiler_params=LIMIT,
        cost_estimate=cost(rows, heads),
        name="key_type",
    )(*in_hbm(*pieces[:-8]), *late, *in_hbm(w_query, w_key), own, twin)


def query_part(x, s, t, heads, chosen):
    rows, width = x.shape
    stud = s.shape[1] // heads
    score = pltpu.VMEM((rows, rows), jnp.float32)
    return pl.pallas_call(
        functools.partial(query_kernel, heads=heads, chosen=chosen, block=math.gcd(rows, 256)),
        out_shape=jax.ShapeDtypeStruct((len(chosen) * stud, width), jnp.bfloat16),
        in_specs=[HBM, VMEM, VMEM],
        out_specs=VMEM,
        scratch_shapes=[
            pltpu.VMEM(x.shape, jnp.bfloat16),
            score,
            score,
            pltpu.VMEM(s.shape, jnp.float32),
            pltpu.VMEM(s.shape[::-1], jnp.float32),
            pltpu.SemaphoreType.DMA,
        ],
        compiler_params=LIMIT,
        cost_estimate=cost(rows, len(chosen)),
        name="query_type",
    )(*in_hbm(x), *in_vmem(s), t)


def by_sequence(teacher_q, teacher_k, student_in, w_query, w_key):
    places = lax.axis_size("ctx")
    levels = places // 4
    heads = HEADS // places
    index = lax.axis_index("head")
    own_k, own_x = (lax.dynamic_index_in_dim(value, index, 0, False) for value in (teacher_k, student_in))
    tokens = own_x.shape[0]

    ring = [2 * k for k in range(levels)] + [2 * k + 1 for k in reversed(range(levels))]
    count = len(ring)
    forward, backward, twin = [], [], []
    for position in range(count):
        for core in range(2):
            here = ring[position] * 2 + core
            forward.append((here, ring[(position + 1) % count] * 2 + core))
            backward.append((here, ring[position - 1] * 2 + core))
            twin.append((here, here ^ 1))

    pieces, spots = [], []

    def keep(value, step, offset=0):
        pieces.extend((value, lax.ppermute(value, "ctx", twin)))
        spots.extend(((step, 0, offset), (step, 1, offset)))

    where = lax.axis_index("ctx")
    level, side = where // 4, where // 2 % 2
    width = own_k.shape[1] // levels
    keys = []
    for other in range(levels):
        piece = lax.dynamic_slice_in_dim(own_k, (level ^ other) * width, width, 1)
        if other:
            piece = lax.ppermute(piece, "ctx", [(i, i ^ (4 * other)) for i in range(places)])
        keys.append(piece)

    def across(keys):
        low, high = keys[:, : width // 2], keys[:, width // 2 :]
        stay, leave = jnp.where(side == 1, high, low), jnp.where(side == 1, low, high)
        got = lax.ppermute(leave, "ctx", [(i, i ^ 2) for i in range(places)])
        return jnp.concatenate([stay, got])

    half = tokens // 2
    parts = split(teacher_q, places)
    keep(own_x, 0)
    ahead = behind = own_x
    for step in range(1, count // 2):
        ahead = lax.ppermute(ahead, "ctx", forward)
        behind = lax.ppermute(behind, "ctx", backward)
        keep(ahead, -step)
        keep(behind, step)
        if step == count // 2 - 2:
            ahead, behind, keys = lax.optimization_barrier((ahead, behind, keys))
            keys = across(jnp.concatenate(keys))
    ahead = lax.ppermute(ahead[:half], "ctx", forward)
    behind = lax.ppermute(behind[half:], "ctx", backward)
    keep(ahead, -(count // 2))
    keep(behind, count // 2, half)
    twin_keys = lax.ppermute(keys, "ctx", twin)

    parts, _, keys = lax.optimization_barrier((parts, (ahead, behind), keys))
    tq = lax.all_to_all(parts, "ctx", 0, 0, tiled=True).reshape(places * tokens, parts.shape[2])

    x, s, part_k = key_part(pieces, spots, w_query, w_key, keys, twin_keys, heads)

    def swap(part):
        return lax.ppermute(part, "head", [(0, 1), (1, 0)])

    def both(part, other):
        return part.astype(jnp.float32) + other.astype(jnp.float32)

    first, last = (tuple(range(lo, lo + heads // 2)) for lo in (0, heads // 2))
    other_k = swap(part_k)
    part = query_part(x, s, tq, heads, first)
    other = swap(part)
    s, part = lax.optimization_barrier((s, part))
    part_last = query_part(x, s, tq, heads, last)
    other_last = swap(part_last)
    other_k, other, part_last = lax.optimization_barrier((other_k, other, part_last))
    grad_q = jnp.pad(both(part, other), ((0, part_last.shape[0]), (0, 0)))
    grad_q = lax.dynamic_update_slice(grad_q, both(part_last, other_last), (part.shape[0], 0))
    return grad_q, both(part_k, other_k)


def score_tile(local_part, key_part, offset, tile_width, head_width):
    key_tile = lax.dynamic_slice_in_dim(key_part, offset, tile_width, 2)
    product = lax.dot_general(
        local_part, key_tile, (((1,), (1,)), ((0,), (0,))), preferred_element_type=jnp.float32
    )
    return product / math.sqrt(head_width)


def by_rows(teacher_q, teacher_k, student_in, w_query, w_key):
    query_width = DTQ // HEADS
    key_width = DTK // HEADS
    stud_width = DS // HEADS
    batch_count = teacher_q.shape[0]
    share = teacher_q.shape[1] // lax.axis_size("head")
    first = lax.axis_index("head") * share
    own_query = lax.dynamic_slice_in_dim(teacher_q, first, share, 1)
    own_key = lax.dynamic_slice_in_dim(teacher_k, first, share, 1)
    own_input = lax.dynamic_slice_in_dim(student_in, first, share, 1)
    teach_query, teach_key = (
        lax.all_to_all(
            own_query.transpose(2, 0, 1), "ctx", split_axis=0, concat_axis=2, tiled=True
        ),
        lax.all_to_all(own_key.transpose(2, 0, 1), "ctx", split_axis=0, concat_axis=2, tiled=True),
    )
    student_rows = lax.all_gather(own_input, "ctx", axis=1, tiled=True)
    row_count = student_rows.shape[1]
    across = (((1,), (2,)), ((), ()))
    stud_query = lax.dot_general(
        w_query, student_rows, across, preferred_element_type=jnp.float32
    ).astype(jnp.bfloat16)
    stud_key = lax.dot_general(
        w_key, student_rows, across, preferred_element_type=jnp.float32
    ).astype(jnp.bfloat16)
    heads_here = stud_query.shape[0] // stud_width
    gathered_all = (
        lax.all_gather(teach_query, "head", axis=2, tiled=True),
        lax.all_gather(teach_key, "head", axis=2, tiled=True),
        lax.all_gather(stud_query, "head", axis=2, tiled=True),
        lax.all_gather(stud_key, "head", axis=2, tiled=True),
    )
    own_all = (teach_query, teach_key, stud_query, stud_key)
    key_count = gathered_all[0].shape[2]
    widths = (query_width, key_width, stud_width, stud_width)
    tile_width = math.gcd(key_count, 512)
    tile_count = key_count // tile_width
    tiles = jnp.arange(tile_count)
    batched = (((2,), (2,)), ((0,), (0,)))
    weight_query = jnp.zeros((heads_here * stud_width, w_query.shape[1]), jnp.float32)
    weight_key = jnp.zeros((heads_here * stud_width, w_key.shape[1]), jnp.float32)
    for index in range(batch_count):
        local_parts = tuple(
            (
                own_all[member][:, index, :].reshape(heads_here, widths[member], row_count)
                for member in range(4)
            )
        )
        key_parts = tuple(
            (
                gathered_all[member][:, index, :].reshape(heads_here, widths[member], key_count)
                for member in range(4)
            )
        )

        def stat_step(state_now, tile_index):
            offset = tile_index * tile_width
            updated = []
            for member in range(4):
                running_max, running_sum = state_now[member]
                scores = score_tile(
                    local_parts[member], key_parts[member], offset, tile_width, widths[member]
                )
                new_max = jnp.maximum(running_max, jnp.max(scores, axis=2))
                running_sum = running_sum * jnp.exp(running_max - new_max) + jnp.sum(
                    jnp.exp(scores - new_max[:, :, None]), axis=2
                )
                updated.append((new_max, running_sum))
            return (tuple(updated), None)

        start_stats = tuple(
            (
                (
                    jnp.full((heads_here, row_count), -jnp.inf, jnp.float32),
                    jnp.zeros((heads_here, row_count), jnp.float32),
                )
                for member in range(4)
            )
        )
        final_stats, unused = lax.scan(stat_step, start_stats, tiles)
        log_totals = tuple(
            (final_stats[member][0] + jnp.log(final_stats[member][1]) for member in range(4))
        )
        zero_terms = jnp.zeros((heads_here, stud_width, row_count), jnp.float32)

        def grad_step(state_now, tile_index):
            offset = tile_index * tile_width
            scores = [
                score_tile(
                    local_parts[member], key_parts[member], offset, tile_width, widths[member]
                )
                for member in range(4)
            ]
            row_probs = [
                jnp.exp(scores[member] - log_totals[member][:, :, None]) for member in range(4)
            ]
            differences = (
                (row_probs[2] - row_probs[0]).astype(jnp.bfloat16),
                (row_probs[3] - row_probs[1]).astype(jnp.bfloat16),
            )
            key_tiles = (
                lax.dynamic_slice_in_dim(key_parts[2], offset, tile_width, 2),
                lax.dynamic_slice_in_dim(key_parts[3], offset, tile_width, 2),
            )
            row_terms = tuple(
                (
                    state_now[member]
                    + lax.dot_general(
                        key_tiles[member],
                        differences[member],
                        batched,
                        preferred_element_type=jnp.float32,
                    )
                    for member in range(2)
                )
            )
            contrib = tuple(
                (
                    lax.dot_general(
                        local_parts[2 + member],
                        differences[member],
                        (((2,), (1,)), ((0,), (0,))),
                        preferred_element_type=jnp.float32,
                    )
                    for member in range(2)
                )
            )
            return (row_terms, contrib)

        sums, pieces = lax.scan(grad_step, (zero_terms, zero_terms), tiles)
        row_query, row_key = sums
        spread = tuple(
            (
                pieces[member].transpose(1, 2, 0, 3).reshape(heads_here, stud_width, key_count)
                for member in range(2)
            )
        )
        col_query, col_key = (
            lax.psum_scatter(
                spread[0].astype(jnp.bfloat16), "head", scatter_dimension=2, tiled=True
            ).astype(jnp.float32),
            lax.psum_scatter(
                spread[1].astype(jnp.bfloat16), "head", scatter_dimension=2, tiled=True
            ).astype(jnp.float32),
        )
        query_grad = (
            ((row_query + col_query) / math.sqrt(stud_width))
            .astype(jnp.bfloat16)
            .reshape(heads_here * stud_width, row_count)
        )
        key_grad = (
            ((row_key + col_key) / math.sqrt(stud_width))
            .astype(jnp.bfloat16)
            .reshape(heads_here * stud_width, row_count)
        )
        weight_query = weight_query + lax.dot_general(
            query_grad,
            student_rows[index],
            (((1,), (0,)), ((), ())),
            preferred_element_type=jnp.float32,
        )
        weight_key = weight_key + lax.dot_general(
            key_grad,
            student_rows[index],
            (((1,), (0,)), ((), ())),
            preferred_element_type=jnp.float32,
        )
    grad_query, grad_key = (
        lax.psum(weight_query.astype(jnp.bfloat16), "head").astype(jnp.float32),
        lax.psum(weight_key.astype(jnp.bfloat16), "head").astype(jnp.float32),
    )
    return (grad_query, grad_key)


def solution(mesh):
    placed = (
        P(None, "ctx", None),
        P(None, "ctx", None),
        P(None, "ctx", None),
        P("ctx", None),
        P("ctx", None),
    )
    places = mesh.shape["ctx"]

    def on_device(*args):
        batch, tokens, _ = args[0].shape
        even = places in (8, 16, 32) and tokens % 32 == 0
        if even and batch == mesh.shape["head"] == 2 and tokens * places <= 1024:
            return by_sequence(*args)
        return by_rows(*args)

    return jax.shard_map(
        on_device,
        mesh=mesh,
        in_specs=placed,
        out_specs=(P("ctx", None), P("ctx", None)),
        check_vma=False,
    )
```

```python
import functools
import math

import jax
import jax.numpy as jnp
from jax import lax
from jax.experimental import pallas as pl
from jax.experimental.pallas import tpu as pltpu
from jax.sharding import PartitionSpec as P

DTQ = 8192
DTK = 1024
DS = 2048
HEADS = 64
LOG2E = 1.4426950408889634
SPREAD = 80.0


def dot(a, b, ca, cb):
    return lax.dot_general(a, b, (((ca,), (cb,)), ((), ())), preferred_element_type=jnp.float32)


def rows_in(index, block):
    return pl.ds(index * block, block)


def masked(value, head, width):
    lane = lax.broadcasted_iota(jnp.int32, value.shape, 1)
    keep = (lane >= head * width) & (lane < (head + 1) * width)
    return jnp.where(keep, value, jnp.zeros_like(value))


def norms(ref, width, chosen):
    first, last = chosen[0], chosen[-1] + 1
    if (first * width) % 128 == 0 and (last * width) % 128 == 0:
        value = ref[:, first * width : last * width].astype(jnp.float32)
    else:
        value, first = ref[...].astype(jnp.float32), 0
    square = (value * value).astype(jnp.bfloat16)
    column = lax.broadcasted_iota(jnp.int32, (square.shape[1], 128), 0) + first * width
    lane = lax.broadcasted_iota(jnp.int32, (square.shape[1], 128), 1)
    member = ((column >= lane * width) & (column < (lane + 1) * width)).astype(jnp.bfloat16)
    total = dot(square, member, 1, 0)
    factor = LOG2E / math.sqrt(width)
    high = jnp.max(total, axis=0, keepdims=True) * (factor * (1 + 2**-6))
    low = jnp.min(total, axis=0, keepdims=True) * (factor * (1 - 2**-6))
    lane = lax.broadcasted_iota(jnp.int32, (1, 128), 1)
    gap = jnp.where((lane >= chosen[0]) & (lane < last), high - low, 0.0)
    return high, jnp.max(gap)


def gradients(t_ref, s_ref, et_ref, es_ref, g_ref, gt_ref, *, heads, chosen, teach, block):
    rows, feats = s_ref.shape
    blocks = rows // block
    stud = feats // heads
    factors = tuple(LOG2E / math.sqrt(width) for width in (teach, stud))
    aligned = teach % 128 == 0

    def teacher(index, head):
        if aligned:
            part = t_ref.at[:, pl.ds(head * teach, teach)]
            return part[rows_in(index, block), :], part[...]
        return masked(t_ref[rows_in(index, block), :], head, teach), t_ref[...]

    def student(index, head):
        return masked(s_ref[rows_in(index, block), :], head, stud), s_ref[...]

    g_ref[...] = jnp.zeros_like(g_ref)
    gt_ref[...] = jnp.zeros_like(gt_ref)
    top_t, gap_t = norms(t_ref, teach, chosen)
    top_s, gap_s = norms(s_ref, stud, chosen)
    safe = jnp.maximum(gap_t, gap_s) < SPREAD

    @pl.when(safe)
    def _():
        flipped = s_ref[...].T
        for head in chosen:
            pick = slice(head, head + 1)
            sums = []
            for own, e_ref, factor, top in (
                (teacher, et_ref, factors[0], top_t[:, pick]),
                (student, es_ref, factors[1], top_s[:, pick]),
            ):
                down = [jnp.zeros((1, block), jnp.float32) for _ in range(blocks)]
                along = []
                for index in range(blocks):
                    left, right = own(index, head)
                    lo = index * block
                    e = jnp.exp2(dot(left, right[lo:], 1, 1) * factor - top)
                    e_ref[rows_in(index, block), lo:] = e
                    for other in range(index, blocks):
                        part = e[:, other * block - lo : (other + 1) * block - lo]
                        down[other] = down[other] + jnp.sum(part, axis=0, keepdims=True)
                    width = math.gcd(block, 128)
                    parts = [e[:, at : at + width] for at in range(block, e.shape[1], width)]
                    along.append(sum(parts) if parts else jnp.zeros((block, width), jnp.float32))
                along = jnp.sum(jnp.concatenate(along, axis=0).T, axis=0, keepdims=True)
                sums.append(jnp.concatenate(down, axis=1) + along)
            across = [1.0 / total for total in sums]
            down = [jnp.broadcast_to(a, (128, rows)).T[:, :1] for a in across]
            right = masked(s_ref[...], head, stud)
            for index in range(blocks):
                lo = index * block
                here = rows_in(index, block)
                h = es_ref[here, lo:] * (down[1][lo : lo + block] + across[1][:, lo:])
                h = h - et_ref[here, lo:] * (down[0][lo : lo + block] + across[0][:, lo:])
                h = h.astype(jnp.bfloat16)
                g_ref[here, :] += dot(h, right[lo:], 1, 0)
                if index < blocks - 1:
                    feats_here = slice(head * stud, (head + 1) * stud)
                    left = flipped[feats_here, lo : lo + block]
                    gt_ref[feats_here, lo + block :] += dot(left, h[:, block:], 1, 0)

    @pl.when(jnp.logical_not(safe))
    def _():
        for head in chosen:

            def step(index, carry):
                here = rows_in(index, block)
                probs = []
                for k, own in enumerate((teacher, student)):
                    left, right = own(index, head)
                    score = dot(left, right, 1, 1) * (factors[k] / LOG2E)
                    e = jnp.exp(score - jnp.max(score, axis=1, keepdims=True))
                    probs.append(e / jnp.sum(e, axis=1, keepdims=True))
                difference = probs[1] - probs[0]
                right = masked(s_ref[...], head, stud)
                g_ref[here, :] += dot(difference.astype(jnp.bfloat16), right, 1, 0)
                left = masked(s_ref[here, :], head, stud)
                g_ref[...] += dot(difference.T.astype(jnp.bfloat16), left, 1, 0)
                return carry

            lax.fori_loop(0, blocks, step, 0)


def weight_grad(g_ref, gt_ref, x_ref, o_ref, first, stud):
    grad = ((g_ref[...].T + gt_ref[...]) * (1.0 / math.sqrt(stud))).astype(jnp.bfloat16)
    grad = grad[first : first + o_ref.shape[0]]
    columns = math.gcd(x_ref.shape[1], 512)
    for lo in range(0, x_ref.shape[1], columns):
        part = pl.ds(lo, columns)
        o_ref[:, part] = dot(grad, x_ref[:, part], 1, 0).astype(jnp.bfloat16)


def split_kernel(t_ref, o_ref, sems):
    own = t_ref.at[lax.axis_index("head")]
    places, _, width = o_ref.shape
    copies = [
        pltpu.make_async_copy(own.at[:, pl.ds(place * width, width)], o_ref.at[place], sems.at[place])
        for place in range(places)
    ]
    for copy in copies:
        copy.start()
    for copy in copies:
        copy.wait()


def split(t, places):
    return pl.pallas_call(
        split_kernel,
        out_shape=jax.ShapeDtypeStruct((places, t.shape[1], t.shape[2] // places), t.dtype),
        in_specs=[HBM],
        out_specs=VMEM,
        scratch_shapes=[pltpu.SemaphoreType.DMA((places,))],
        name="split",
    )(t)


def key_kernel(*refs, spots, heads, teach, block):
    count = len(spots)
    pieces, refs = refs[:count], refs[count:]
    wq_hbm, wk_hbm, own_ref, twin_ref, x_hbm, sq_ref, sk_ref, t_ref, o_ref, *refs = refs
    x_ref, wq_ref, wk_ref, et_ref, es_ref, g_ref, gt_ref, sems = refs
    places = lax.axis_size("ctx")
    where = lax.axis_index("ctx")
    levels = places // 4
    rows = x_ref.shape[0]
    tokens = rows // places
    chip, core = where // 2, where % 2
    level, side = chip // 2, chip % 2
    position = jnp.where(side == 0, level, 2 * levels - 1 - level)
    copies = []
    for number, (piece, (step, twin, offset)) in enumerate(zip(pieces, spots)):
        other = (position + step + 2 * levels) % (2 * levels)
        other = jnp.where(other < levels, 2 * other, 2 * (2 * levels - 1 - other) + 1)
        row = pl.multiple_of((other * 2 + (core + twin) % 2) * tokens + offset, piece.shape[0])
        target = x_ref.at[pl.ds(row, piece.shape[0]), :]
        copies.append(pltpu.make_async_copy(piece, target, sems.at[number]))
    for number, (source, target) in enumerate(((wq_hbm, wq_ref), (wk_hbm, wk_ref))):
        copies.append(pltpu.make_async_copy(source, target, sems.at[count + number]))
    for copy in copies:
        copy.start()
    chips = places // 2
    for twin, ref in enumerate((own_ref, twin_ref)):
        part = ref[...].astype(jnp.float32)
        part = jnp.where(core == 1, pltpu.roll(part, part.shape[1] // 2, 1), part).astype(jnp.bfloat16)
        for number in range(chips):
            row = ((chip ^ (2 * (number % levels) + number // levels)) * 2 + (core + twin) % 2) * tokens
            here = pl.ds(pl.multiple_of(row, tokens), tokens)
            t_ref[here, :] = part[number * tokens : (number + 1) * tokens]
    for copy in copies:
        copy.wait()
    leave = pltpu.make_async_copy(x_ref, x_hbm, sems.at[0])
    leave.start()
    for index in range(rows // block):
        here = rows_in(index, block)
        sq_ref[here, :] = dot(x_ref[here, :], wq_ref[...], 1, 1).astype(jnp.bfloat16)
        sk_ref[here, :] = dot(x_ref[here, :], wk_ref[...], 1, 1).astype(jnp.bfloat16)
    gradients(
        t_ref,
        sk_ref,
        et_ref,
        es_ref,
        g_ref,
        gt_ref,
        heads=heads,
        chosen=range(heads // 2),
        teach=teach,
        block=block,
    )
    weight_grad(g_ref, gt_ref, x_ref, o_ref, 0, wk_ref.shape[0] // heads)
    leave.wait()


def half_kernel(
    x_hbm, s_ref, t_ref, o_ref, x_ref, et_ref, es_ref, g_ref, gt_ref, sem, *, heads, chosen, teach, block
):
    fetch = pltpu.make_async_copy(x_hbm, x_ref, sem)
    fetch.start()
    stud = s_ref.shape[1] // heads
    gradients(
        t_ref,
        s_ref,
        et_ref,
        es_ref,
        g_ref,
        gt_ref,
        heads=heads,
        chosen=chosen,
        teach=teach,
        block=block,
    )
    fetch.wait()
    weight_grad(g_ref, gt_ref, x_ref, o_ref, chosen[0] * stud, stud)


def cost(rows, heads):
    return pl.CostEstimate(
        flops=2 * rows * rows * 256 * 3 * heads,
        bytes_accessed=4 * rows * rows,
        transcendentals=2 * rows * rows * heads,
    )


VMEM = pl.BlockSpec(memory_space=pltpu.VMEM)
HBM = pl.BlockSpec(memory_space=pltpu.HBM)
LIMIT = pltpu.CompilerParams(vmem_limit_bytes=20 * 2**20)


def in_hbm(*values):
    return [pltpu.with_memory_space_constraint(value, pltpu.HBM) for value in values]


def in_vmem(*values):
    return [pltpu.with_memory_space_constraint(value, pltpu.VMEM) for value in values]


def key_part(pieces, spots, w_query, w_key, own, twin, heads):
    feats, width = w_key.shape
    rows = 2 * own.shape[0]
    score = pltpu.VMEM((rows, rows), jnp.float32)
    late = [put(value) for put, value in zip((in_hbm, in_vmem) * 2 + (in_vmem,) * 4, pieces[-8:])]
    late = [value for (value,) in late]
    kept = [HBM] * (len(pieces) - 8) + [HBM, VMEM] * 2 + [VMEM] * 4
    return pl.pallas_call(
        functools.partial(
            key_kernel,
            spots=tuple(spots),
            heads=heads,
            teach=own.shape[1] // 2 // heads,
            block=math.gcd(rows, 256),
        ),
        out_shape=(
            pltpu.HBM((rows, width), jnp.bfloat16),
            pltpu.VMEM((rows, feats), jnp.bfloat16),
            pltpu.VMEM((rows, feats), jnp.bfloat16),
            pltpu.VMEM((rows, own.shape[1]), jnp.bfloat16),
            jax.ShapeDtypeStruct((feats // 2, width), jnp.bfloat16),
        ),
        in_specs=kept + [HBM] * 2 + [VMEM] * 2,
        out_specs=(HBM, VMEM, VMEM, VMEM, VMEM),
        scratch_shapes=[
            pltpu.VMEM((rows, width), jnp.bfloat16),
            pltpu.VMEM(w_query.shape, jnp.bfloat16),
            pltpu.VMEM(w_key.shape, jnp.bfloat16),
            score,
            score,
            pltpu.VMEM((rows, feats), jnp.float32),
            pltpu.VMEM((feats, rows), jnp.float32),
            pltpu.SemaphoreType.DMA((len(pieces) + 2,)),
        ],
        compiler_params=LIMIT,
        cost_estimate=cost(rows, heads // 2),
        name="first_keys",
    )(*in_hbm(*pieces[:-8]), *late, *in_hbm(w_query, w_key), own, twin)


def half_part(x, s, t, heads, chosen, teach):
    rows, width = x.shape
    stud = s.shape[1] // heads
    score = pltpu.VMEM((rows, rows), jnp.float32)
    return pl.pallas_call(
        functools.partial(
            half_kernel, heads=heads, chosen=chosen, teach=teach, block=math.gcd(rows, 256)
        ),
        out_shape=jax.ShapeDtypeStruct((len(chosen) * stud, width), jnp.bfloat16),
        in_specs=[HBM, VMEM, VMEM],
        out_specs=VMEM,
        scratch_shapes=[
            pltpu.VMEM(x.shape, jnp.bfloat16),
            score,
            score,
            pltpu.VMEM(s.shape, jnp.float32),
            pltpu.VMEM(s.shape[::-1], jnp.float32),
            pltpu.SemaphoreType.DMA,
        ],
        compiler_params=LIMIT,
        cost_estimate=cost(rows, len(chosen)),
        name="half_type",
    )(*in_hbm(x), *in_vmem(s), t)


def by_sequence(teacher_q, teacher_k, student_in, w_query, w_key):
    places = lax.axis_size("ctx")
    levels = places // 4
    heads = HEADS // places
    index = lax.axis_index("head")
    own_k, own_x = (lax.dynamic_index_in_dim(value, index, 0, False) for value in (teacher_k, student_in))
    tokens = own_x.shape[0]

    ring = [2 * k for k in range(levels)] + [2 * k + 1 for k in reversed(range(levels))]
    count = len(ring)
    forward, backward, twin = [], [], []
    for position in range(count):
        for core in range(2):
            here = ring[position] * 2 + core
            forward.append((here, ring[(position + 1) % count] * 2 + core))
            backward.append((here, ring[position - 1] * 2 + core))
            twin.append((here, here ^ 1))

    pieces, spots = [], []

    def keep(value, step, offset=0):
        pieces.extend((value, lax.ppermute(value, "ctx", twin)))
        spots.extend(((step, 0, offset), (step, 1, offset)))

    where = lax.axis_index("ctx")
    level, side = where // 4, where // 2 % 2
    width = own_k.shape[1] // levels
    keys = []
    for other in range(levels):
        piece = lax.dynamic_slice_in_dim(own_k, (level ^ other) * width, width, 1)
        if other:
            piece = lax.ppermute(piece, "ctx", [(i, i ^ (4 * other)) for i in range(places)])
        keys.append(piece)

    def across(keys):
        low, high = keys[:, : width // 2], keys[:, width // 2 :]
        stay, leave = jnp.where(side == 1, high, low), jnp.where(side == 1, low, high)
        got = lax.ppermute(leave, "ctx", [(i, i ^ 2) for i in range(places)])
        return jnp.concatenate([stay, got])

    half = tokens // 2
    parts = split(teacher_q, places)
    keep(own_x, 0)
    ahead = behind = own_x
    for step in range(1, count // 2):
        ahead = lax.ppermute(ahead, "ctx", forward)
        behind = lax.ppermute(behind, "ctx", backward)
        keep(ahead, -step)
        keep(behind, step)
        if step == count // 2 - 2:
            ahead, behind, keys = lax.optimization_barrier((ahead, behind, keys))
            keys = across(jnp.concatenate(keys))
    ahead = lax.ppermute(ahead[:half], "ctx", forward)
    behind = lax.ppermute(behind[half:], "ctx", backward)
    keep(ahead, -(count // 2))
    keep(behind, count // 2, half)
    twin_keys = lax.ppermute(keys, "ctx", twin)

    parts, _, keys = lax.optimization_barrier((parts, (ahead, behind), keys))
    tq = lax.all_to_all(parts, "ctx", 0, 0, tiled=True).reshape(places * tokens, parts.shape[2])

    x, s, keys_s, keys_t, part_k = key_part(pieces, spots, w_query, w_key, keys, twin_keys, heads)

    def swap(part):
        return lax.ppermute(part, "head", [(0, 1), (1, 0)])

    def both(part, other):
        return part.astype(jnp.float32) + other.astype(jnp.float32)

    first, last = (tuple(range(lo, lo + heads // 2)) for lo in (0, heads // 2))
    swapped = [(part_k, swap(part_k))]
    for stud, teach, chosen in ((keys_s, keys_t, last), (s, tq, first), *((s, tq, (head,)) for head in last)):
        stud, part = lax.optimization_barrier((stud, swapped[-1][0]))
        swapped[-1] = (part, swapped[-1][1])
        width = DTK if teach is keys_t else DTQ
        part = half_part(x, stud, teach, heads, chosen, width // HEADS)
        swapped.append((part, swap(part)))
    part, other = swapped[-1]
    part, swapped[:-1] = lax.optimization_barrier((part, swapped[:-1]))
    grad_k = jnp.concatenate([both(*pair) for pair in swapped[:2]])
    other, grad_k = lax.optimization_barrier((other, grad_k))
    swapped[-1] = (part, other)
    return jnp.concatenate([both(*pair) for pair in swapped[2:]]), grad_k


def score_tile(local_part, key_part, offset, tile_width, head_width):
    key_tile = lax.dynamic_slice_in_dim(key_part, offset, tile_width, 2)
    product = lax.dot_general(
        local_part, key_tile, (((1,), (1,)), ((0,), (0,))), preferred_element_type=jnp.float32
    )
    return product / math.sqrt(head_width)


def by_rows(teacher_q, teacher_k, student_in, w_query, w_key):
    query_width = DTQ // HEADS
    key_width = DTK // HEADS
    stud_width = DS // HEADS
    batch_count = teacher_q.shape[0]
    share = teacher_q.shape[1] // lax.axis_size("head")
    first = lax.axis_index("head") * share
    own_query = lax.dynamic_slice_in_dim(teacher_q, first, share, 1)
    own_key = lax.dynamic_slice_in_dim(teacher_k, first, share, 1)
    own_input = lax.dynamic_slice_in_dim(student_in, first, share, 1)
    teach_query, teach_key = (
        lax.all_to_all(
            own_query.transpose(2, 0, 1), "ctx", split_axis=0, concat_axis=2, tiled=True
        ),
        lax.all_to_all(own_key.transpose(2, 0, 1), "ctx", split_axis=0, concat_axis=2, tiled=True),
    )
    student_rows = lax.all_gather(own_input, "ctx", axis=1, tiled=True)
    row_count = student_rows.shape[1]
    across = (((1,), (2,)), ((), ()))
    stud_query = lax.dot_general(
        w_query, student_rows, across, preferred_element_type=jnp.float32
    ).astype(jnp.bfloat16)
    stud_key = lax.dot_general(
        w_key, student_rows, across, preferred_element_type=jnp.float32
    ).astype(jnp.bfloat16)
    heads_here = stud_query.shape[0] // stud_width
    gathered_all = (
        lax.all_gather(teach_query, "head", axis=2, tiled=True),
        lax.all_gather(teach_key, "head", axis=2, tiled=True),
        lax.all_gather(stud_query, "head", axis=2, tiled=True),
        lax.all_gather(stud_key, "head", axis=2, tiled=True),
    )
    own_all = (teach_query, teach_key, stud_query, stud_key)
    key_count = gathered_all[0].shape[2]
    widths = (query_width, key_width, stud_width, stud_width)
    tile_width = math.gcd(key_count, 512)
    tile_count = key_count // tile_width
    tiles = jnp.arange(tile_count)
    batched = (((2,), (2,)), ((0,), (0,)))
    weight_query = jnp.zeros((heads_here * stud_width, w_query.shape[1]), jnp.float32)
    weight_key = jnp.zeros((heads_here * stud_width, w_key.shape[1]), jnp.float32)
    for index in range(batch_count):
        local_parts = tuple(
            (
                own_all[member][:, index, :].reshape(heads_here, widths[member], row_count)
                for member in range(4)
            )
        )
        key_parts = tuple(
            (
                gathered_all[member][:, index, :].reshape(heads_here, widths[member], key_count)
                for member in range(4)
            )
        )

        def stat_step(state_now, tile_index):
            offset = tile_index * tile_width
            updated = []
            for member in range(4):
                running_max, running_sum = state_now[member]
                scores = score_tile(
                    local_parts[member], key_parts[member], offset, tile_width, widths[member]
                )
                new_max = jnp.maximum(running_max, jnp.max(scores, axis=2))
                running_sum = running_sum * jnp.exp(running_max - new_max) + jnp.sum(
                    jnp.exp(scores - new_max[:, :, None]), axis=2
                )
                updated.append((new_max, running_sum))
            return (tuple(updated), None)

        start_stats = tuple(
            (
                (
                    jnp.full((heads_here, row_count), -jnp.inf, jnp.float32),
                    jnp.zeros((heads_here, row_count), jnp.float32),
                )
                for member in range(4)
            )
        )
        final_stats, unused = lax.scan(stat_step, start_stats, tiles)
        log_totals = tuple(
            (final_stats[member][0] + jnp.log(final_stats[member][1]) for member in range(4))
        )
        zero_terms = jnp.zeros((heads_here, stud_width, row_count), jnp.float32)

        def grad_step(state_now, tile_index):
            offset = tile_index * tile_width
            scores = [
                score_tile(
                    local_parts[member], key_parts[member], offset, tile_width, widths[member]
                )
                for member in range(4)
            ]
            row_probs = [
                jnp.exp(scores[member] - log_totals[member][:, :, None]) for member in range(4)
            ]
            differences = (
                (row_probs[2] - row_probs[0]).astype(jnp.bfloat16),
                (row_probs[3] - row_probs[1]).astype(jnp.bfloat16),
            )
            key_tiles = (
                lax.dynamic_slice_in_dim(key_parts[2], offset, tile_width, 2),
                lax.dynamic_slice_in_dim(key_parts[3], offset, tile_width, 2),
            )
            row_terms = tuple(
                (
                    state_now[member]
                    + lax.dot_general(
                        key_tiles[member],
                        differences[member],
                        batched,
                        preferred_element_type=jnp.float32,
                    )
                    for member in range(2)
                )
            )
            contrib = tuple(
                (
                    lax.dot_general(
                        local_parts[2 + member],
                        differences[member],
                        (((2,), (1,)), ((0,), (0,))),
                        preferred_element_type=jnp.float32,
                    )
                    for member in range(2)
                )
            )
            return (row_terms, contrib)

        sums, pieces = lax.scan(grad_step, (zero_terms, zero_terms), tiles)
        row_query, row_key = sums
        spread = tuple(
            (
                pieces[member].transpose(1, 2, 0, 3).reshape(heads_here, stud_width, key_count)
                for member in range(2)
            )
        )
        col_query, col_key = (
            lax.psum_scatter(
                spread[0].astype(jnp.bfloat16), "head", scatter_dimension=2, tiled=True
            ).astype(jnp.float32),
            lax.psum_scatter(
                spread[1].astype(jnp.bfloat16), "head", scatter_dimension=2, tiled=True
            ).astype(jnp.float32),
        )
        query_grad = (
            ((row_query + col_query) / math.sqrt(stud_width))
            .astype(jnp.bfloat16)
            .reshape(heads_here * stud_width, row_count)
        )
        key_grad = (
            ((row_key + col_key) / math.sqrt(stud_width))
            .astype(jnp.bfloat16)
            .reshape(heads_here * stud_width, row_count)
        )
        weight_query = weight_query + lax.dot_general(
            query_grad,
            student_rows[index],
            (((1,), (0,)), ((), ())),
            preferred_element_type=jnp.float32,
        )
        weight_key = weight_key + lax.dot_general(
            key_grad,
            student_rows[index],
            (((1,), (0,)), ((), ())),
            preferred_element_type=jnp.float32,
        )
    grad_query, grad_key = (
        lax.psum(weight_query.astype(jnp.bfloat16), "head").astype(jnp.float32),
        lax.psum(weight_key.astype(jnp.bfloat16), "head").astype(jnp.float32),
    )
    return (grad_query, grad_key)


def solution(mesh):
    placed = (
        P(None, "ctx", None),
        P(None, "ctx", None),
        P(None, "ctx", None),
        P("ctx", None),
        P("ctx", None),
    )
    places = mesh.shape["ctx"]

    def on_device(*args):
        batch, tokens, _ = args[0].shape
        even = places in (8, 16, 32) and tokens % 32 == 0
        if even and batch == mesh.shape["head"] == 2 and tokens * places <= 1024:
            return by_sequence(*args)
        return by_rows(*args)

    return jax.shard_map(
        on_device,
        mesh=mesh,
        in_specs=placed,
        out_specs=(P("ctx", None), P("ctx", None)),
        check_vma=False,
    )
```

```python
import functools
import math

import jax
import jax.numpy as jnp
from jax import lax
from jax.experimental import pallas as pl
from jax.experimental.pallas import tpu as pltpu
from jax.sharding import PartitionSpec as P

DTQ = 8192
DTK = 1024
DS = 2048
HEADS = 64
LOG2E = 1.4426950408889634
SPREAD = 80.0


def dot(a, b, ca, cb):
    return lax.dot_general(a, b, (((ca,), (cb,)), ((), ())), preferred_element_type=jnp.float32)


def rows_in(index, block):
    return pl.ds(pl.multiple_of(index * block, block), block)


def masked(value, head, width):
    lane = lax.broadcasted_iota(jnp.int32, value.shape, 1)
    keep = (lane >= head * width) & (lane < (head + 1) * width)
    return jnp.where(keep, value, jnp.zeros_like(value))


def norms(ref, width, chosen):
    first, last = chosen[0], chosen[-1] + 1
    if (first * width) % 128 == 0 and (last * width) % 128 == 0:
        value = ref[:, first * width : last * width].astype(jnp.float32)
    else:
        value, first = ref[...].astype(jnp.float32), 0
    square = (value * value).astype(jnp.bfloat16)
    column = lax.broadcasted_iota(jnp.int32, (square.shape[1], 128), 0) + first * width
    lane = lax.broadcasted_iota(jnp.int32, (square.shape[1], 128), 1)
    member = ((column >= lane * width) & (column < (lane + 1) * width)).astype(jnp.bfloat16)
    total = dot(square, member, 1, 0)
    factor = LOG2E / math.sqrt(width)
    high = jnp.max(total, axis=0, keepdims=True) * (factor * (1 + 2**-6))
    low = jnp.min(total, axis=0, keepdims=True) * (factor * (1 - 2**-6))
    lane = lax.broadcasted_iota(jnp.int32, (1, 128), 1)
    gap = jnp.where((lane >= chosen[0]) & (lane < last), high - low, 0.0)
    return high, jnp.max(gap)


def gradients(t_ref, s_ref, et_ref, es_ref, g_ref, gt_ref, *, heads, chosen, teach, block):
    rows, feats = s_ref.shape
    blocks = rows // block
    stud = feats // heads
    factors = tuple(LOG2E / math.sqrt(width) for width in (teach, stud))
    aligned = teach % 128 == 0

    def teacher(index, head):
        if aligned:
            part = t_ref.at[:, pl.ds(pl.multiple_of(head * teach, 128), teach)]
            return part[rows_in(index, block), :], part[...]
        return masked(t_ref[rows_in(index, block), :], head, teach), t_ref[...]

    def student(index, head):
        return masked(s_ref[rows_in(index, block), :], head, stud), s_ref[...]

    g_ref[...] = jnp.zeros_like(g_ref)
    gt_ref[...] = jnp.zeros_like(gt_ref)
    top_t, gap_t = norms(t_ref, teach, chosen)
    top_s, gap_s = norms(s_ref, stud, chosen)
    safe = jnp.maximum(gap_t, gap_s) < SPREAD

    @pl.when(safe)
    def _():
        flipped = s_ref[...].T
        for head in chosen:
            pick = slice(head, head + 1)
            sums = []
            for own, e_ref, factor, top in (
                (teacher, et_ref, factors[0], top_t[:, pick]),
                (student, es_ref, factors[1], top_s[:, pick]),
            ):
                down = [jnp.zeros((1, block), jnp.float32) for _ in range(blocks)]
                along = []
                for index in range(blocks):
                    left, right = own(index, head)
                    lo = index * block
                    e = jnp.exp2(dot(left, right[lo:], 1, 1) * factor - top)
                    e_ref[rows_in(index, block), lo:] = e
                    for other in range(index, blocks):
                        part = e[:, other * block - lo : (other + 1) * block - lo]
                        down[other] = down[other] + jnp.sum(part, axis=0, keepdims=True)
                    width = math.gcd(block, 128)
                    parts = [e[:, at : at + width] for at in range(block, e.shape[1], width)]
                    along.append(sum(parts) if parts else jnp.zeros((block, width), jnp.float32))
                along = jnp.sum(jnp.concatenate(along, axis=0).T, axis=0, keepdims=True)
                sums.append(jnp.concatenate(down, axis=1) + along)
            across = [1.0 / total for total in sums]
            down = [jnp.broadcast_to(a, (128, rows)).T[:, :1] for a in across]
            right = masked(s_ref[...], head, stud)
            for index in range(blocks):
                lo = index * block
                here = rows_in(index, block)
                h = es_ref[here, lo:] * (down[1][lo : lo + block] + across[1][:, lo:])
                h = h - et_ref[here, lo:] * (down[0][lo : lo + block] + across[0][:, lo:])
                h = h.astype(jnp.bfloat16)
                g_ref[here, :] += dot(h, right[lo:], 1, 0)
                if index < blocks - 1:
                    feats_here = slice(head * stud, (head + 1) * stud)
                    left = flipped[feats_here, lo : lo + block]
                    gt_ref[feats_here, lo + block :] += dot(left, h[:, block:], 1, 0)

    @pl.when(jnp.logical_not(safe))
    def _():
        def step(number, carry):
            head, index = chosen[0] + number // blocks, number % blocks
            here = rows_in(index, block)
            probs = []
            for k, own in enumerate((teacher, student)):
                left, right = own(index, head)
                score = dot(left, right, 1, 1) * (factors[k] / LOG2E)
                e = jnp.exp(score - jnp.max(score, axis=1, keepdims=True))
                probs.append(e / jnp.sum(e, axis=1, keepdims=True))
            difference = probs[1] - probs[0]
            right = masked(s_ref[...], head, stud)
            g_ref[here, :] += dot(difference.astype(jnp.bfloat16), right, 1, 0)
            left = masked(s_ref[here, :], head, stud)
            g_ref[...] += dot(difference.T.astype(jnp.bfloat16), left, 1, 0)
            return carry

        lax.fori_loop(0, len(chosen) * blocks, step, 0)


def weight_grad(g_ref, gt_ref, x_ref, o_ref, first, stud):
    grad = ((g_ref[...].T + gt_ref[...]) * (1.0 / math.sqrt(stud))).astype(jnp.bfloat16)
    grad = grad[first : first + o_ref.shape[0]]
    columns = math.gcd(x_ref.shape[1], 512)
    for lo in range(0, x_ref.shape[1], columns):
        part = pl.ds(lo, columns)
        o_ref[:, part] = dot(grad, x_ref[:, part], 1, 0).astype(jnp.bfloat16)


def split_kernel(t_ref, o_ref, sems):
    own = t_ref.at[lax.axis_index("head")]
    places, _, width = o_ref.shape
    copies = [
        pltpu.make_async_copy(own.at[:, pl.ds(place * width, width)], o_ref.at[place], sems.at[place])
        for place in range(places)
    ]
    for copy in copies:
        copy.start()
    for copy in copies:
        copy.wait()


def split(t, places):
    return pl.pallas_call(
        split_kernel,
        out_shape=jax.ShapeDtypeStruct((places, t.shape[1], t.shape[2] // places), t.dtype),
        in_specs=[HBM],
        out_specs=VMEM,
        scratch_shapes=[pltpu.SemaphoreType.DMA((places,))],
        name="split",
    )(t)


def key_kernel(*refs, spots, heads, teach, block):
    count = len(spots)
    pieces, refs = refs[:count], refs[count:]
    wq_hbm, wk_hbm, own_ref, twin_ref, x_hbm, sq_ref, sk_ref, t_ref, o_ref, *refs = refs
    x_ref, wq_ref, wk_ref, et_ref, es_ref, g_ref, gt_ref, sems = refs
    places = lax.axis_size("ctx")
    where = lax.axis_index("ctx")
    levels = places // 4
    rows = x_ref.shape[0]
    tokens = rows // places
    chip, core = where // 2, where % 2
    level, side = chip // 2, chip % 2
    position = jnp.where(side == 0, level, 2 * levels - 1 - level)
    copies = []
    for number, (piece, (step, twin, offset)) in enumerate(zip(pieces, spots)):
        other = (position + step + 2 * levels) % (2 * levels)
        other = jnp.where(other < levels, 2 * other, 2 * (2 * levels - 1 - other) + 1)
        row = pl.multiple_of((other * 2 + (core + twin) % 2) * tokens + offset, piece.shape[0])
        target = x_ref.at[pl.ds(row, piece.shape[0]), :]
        copies.append(pltpu.make_async_copy(piece, target, sems.at[number]))
    for number, (source, target) in enumerate(((wq_hbm, wq_ref), (wk_hbm, wk_ref))):
        copies.append(pltpu.make_async_copy(source, target, sems.at[count + number]))
    for copy in copies:
        copy.start()
    chips = places // 2
    for twin, ref in enumerate((own_ref, twin_ref)):
        part = ref[...].astype(jnp.float32)
        part = jnp.where(core == 1, pltpu.roll(part, part.shape[1] // 2, 1), part).astype(jnp.bfloat16)
        for number in range(chips):
            row = ((chip ^ (2 * (number % levels) + number // levels)) * 2 + (core + twin) % 2) * tokens
            here = pl.ds(pl.multiple_of(row, tokens), tokens)
            t_ref[here, :] = part[number * tokens : (number + 1) * tokens]
    for copy in copies:
        copy.wait()
    leave = pltpu.make_async_copy(x_ref, x_hbm, sems.at[0])
    leave.start()
    for index in range(rows // block):
        here = rows_in(index, block)
        sq_ref[here, :] = dot(x_ref[here, :], wq_ref[...], 1, 1).astype(jnp.bfloat16)
        sk_ref[here, :] = dot(x_ref[here, :], wk_ref[...], 1, 1).astype(jnp.bfloat16)
    gradients(
        t_ref,
        sk_ref,
        et_ref,
        es_ref,
        g_ref,
        gt_ref,
        heads=heads,
        chosen=range(heads // 2),
        teach=teach,
        block=block,
    )
    weight_grad(g_ref, gt_ref, x_ref, o_ref, 0, wk_ref.shape[0] // heads)
    leave.wait()


def half_kernel(
    x_hbm, s_ref, t_ref, o_ref, x_ref, et_ref, es_ref, g_ref, gt_ref, sem, *, heads, chosen, teach, block
):
    fetch = pltpu.make_async_copy(x_hbm, x_ref, sem)
    fetch.start()
    stud = s_ref.shape[1] // heads
    gradients(
        t_ref,
        s_ref,
        et_ref,
        es_ref,
        g_ref,
        gt_ref,
        heads=heads,
        chosen=chosen,
        teach=teach,
        block=block,
    )
    fetch.wait()
    weight_grad(g_ref, gt_ref, x_ref, o_ref, chosen[0] * stud, stud)


def cost(rows, heads):
    return pl.CostEstimate(
        flops=2 * rows * rows * 256 * 3 * heads,
        bytes_accessed=4 * rows * rows,
        transcendentals=2 * rows * rows * heads,
    )


VMEM = pl.BlockSpec(memory_space=pltpu.VMEM)
HBM = pl.BlockSpec(memory_space=pltpu.HBM)
LIMIT = pltpu.CompilerParams(vmem_limit_bytes=20 * 2**20)


def in_hbm(*values):
    return [pltpu.with_memory_space_constraint(value, pltpu.HBM) for value in values]


def in_vmem(*values):
    return [pltpu.with_memory_space_constraint(value, pltpu.VMEM) for value in values]


def key_part(pieces, spots, w_query, w_key, own, twin, heads):
    feats, width = w_key.shape
    rows = 2 * own.shape[0]
    score = pltpu.VMEM((rows, rows), jnp.float32)
    late = [put(value) for put, value in zip((in_hbm, in_vmem) * 2 + (in_vmem,) * 4, pieces[-8:])]
    late = [value for (value,) in late]
    kept = [HBM] * (len(pieces) - 8) + [HBM, VMEM] * 2 + [VMEM] * 4
    return pl.pallas_call(
        functools.partial(
            key_kernel,
            spots=tuple(spots),
            heads=heads,
            teach=own.shape[1] // 2 // heads,
            block=math.gcd(rows, 256),
        ),
        out_shape=(
            pltpu.HBM((rows, width), jnp.bfloat16),
            pltpu.VMEM((rows, feats), jnp.bfloat16),
            pltpu.VMEM((rows, feats), jnp.bfloat16),
            pltpu.VMEM((rows, own.shape[1]), jnp.bfloat16),
            jax.ShapeDtypeStruct((feats // 2, width), jnp.bfloat16),
        ),
        in_specs=kept + [HBM] * 2 + [VMEM] * 2,
        out_specs=(HBM, VMEM, VMEM, VMEM, VMEM),
        scratch_shapes=[
            pltpu.VMEM((rows, width), jnp.bfloat16),
            pltpu.VMEM(w_query.shape, jnp.bfloat16),
            pltpu.VMEM(w_key.shape, jnp.bfloat16),
            score,
            score,
            pltpu.VMEM((rows, feats), jnp.float32),
            pltpu.VMEM((feats, rows), jnp.float32),
            pltpu.SemaphoreType.DMA((len(pieces) + 2,)),
        ],
        compiler_params=LIMIT,
        cost_estimate=cost(rows, heads // 2),
        name="first_keys",
    )(*in_hbm(*pieces[:-8]), *late, *in_hbm(w_query, w_key), own, twin)


def half_part(x, s, t, heads, chosen, teach):
    rows, width = x.shape
    stud = s.shape[1] // heads
    score = pltpu.VMEM((rows, rows), jnp.float32)
    return pl.pallas_call(
        functools.partial(
            half_kernel, heads=heads, chosen=chosen, teach=teach, block=math.gcd(rows, 256)
        ),
        out_shape=jax.ShapeDtypeStruct((len(chosen) * stud, width), jnp.bfloat16),
        in_specs=[HBM, VMEM, VMEM],
        out_specs=VMEM,
        scratch_shapes=[
            pltpu.VMEM(x.shape, jnp.bfloat16),
            score,
            score,
            pltpu.VMEM(s.shape, jnp.float32),
            pltpu.VMEM(s.shape[::-1], jnp.float32),
            pltpu.SemaphoreType.DMA,
        ],
        compiler_params=LIMIT,
        cost_estimate=cost(rows, len(chosen)),
        name="half_type",
    )(*in_hbm(x), *in_vmem(s), t)


def by_sequence(teacher_q, teacher_k, student_in, w_query, w_key):
    places = lax.axis_size("ctx")
    levels = places // 4
    heads = HEADS // places
    index = lax.axis_index("head")
    own_k, own_x = (lax.dynamic_index_in_dim(value, index, 0, False) for value in (teacher_k, student_in))
    tokens = own_x.shape[0]

    ring = [2 * k for k in range(levels)] + [2 * k + 1 for k in reversed(range(levels))]
    count = len(ring)
    forward, backward, twin = [], [], []
    for position in range(count):
        for core in range(2):
            here = ring[position] * 2 + core
            forward.append((here, ring[(position + 1) % count] * 2 + core))
            backward.append((here, ring[position - 1] * 2 + core))
            twin.append((here, here ^ 1))

    pieces, spots = [], []

    def keep(value, step, offset=0):
        pieces.extend((value, lax.ppermute(value, "ctx", twin)))
        spots.extend(((step, 0, offset), (step, 1, offset)))

    where = lax.axis_index("ctx")
    level, side = where // 4, where // 2 % 2
    width = own_k.shape[1] // levels
    keys = []
    for other in range(levels):
        piece = lax.dynamic_slice_in_dim(own_k, (level ^ other) * width, width, 1)
        if other:
            piece = lax.ppermute(piece, "ctx", [(i, i ^ (4 * other)) for i in range(places)])
        keys.append(piece)

    def across(keys):
        low, high = keys[:, : width // 2], keys[:, width // 2 :]
        stay, leave = jnp.where(side == 1, high, low), jnp.where(side == 1, low, high)
        got = lax.ppermute(leave, "ctx", [(i, i ^ 2) for i in range(places)])
        return jnp.concatenate([stay, got])

    half = tokens // 2
    parts = split(teacher_q, places)
    keep(own_x, 0)
    ahead = behind = own_x
    for step in range(1, count // 2):
        ahead = lax.ppermute(ahead, "ctx", forward)
        behind = lax.ppermute(behind, "ctx", backward)
        keep(ahead, -step)
        keep(behind, step)
        if step == count // 2 - 2:
            ahead, behind, keys = lax.optimization_barrier((ahead, behind, keys))
            keys = across(jnp.concatenate(keys))
    ahead = lax.ppermute(ahead[:half], "ctx", forward)
    behind = lax.ppermute(behind[half:], "ctx", backward)
    keep(ahead, -(count // 2))
    keep(behind, count // 2, half)
    twin_keys = lax.ppermute(keys, "ctx", twin)

    parts, _, keys = lax.optimization_barrier((parts, (ahead, behind), keys))
    tq = lax.all_to_all(parts, "ctx", 0, 0, tiled=True).reshape(places * tokens, parts.shape[2])

    x, s, keys_s, keys_t, part_k = key_part(pieces, spots, w_query, w_key, keys, twin_keys, heads)

    def swap(part):
        return lax.ppermute(part, "head", [(0, 1), (1, 0)])

    def both(part, other):
        return part.astype(jnp.float32) + other.astype(jnp.float32)

    first, last = (tuple(range(lo, lo + heads // 2)) for lo in (0, heads // 2))
    swapped = [(part_k, swap(part_k))]
    for stud, teach, chosen in ((keys_s, keys_t, last), (s, tq, first), *((s, tq, (head,)) for head in last)):
        stud, part = lax.optimization_barrier((stud, swapped[-1][0]))
        swapped[-1] = (part, swapped[-1][1])
        width = DTK if teach is keys_t else DTQ
        part = half_part(x, stud, teach, heads, chosen, width // HEADS)
        swapped.append((part, swap(part)))
    part, other = swapped[-1]
    part, swapped[:-1] = lax.optimization_barrier((part, swapped[:-1]))
    grad_k = jnp.concatenate([both(*pair) for pair in swapped[:2]])
    other, grad_k = lax.optimization_barrier((other, grad_k))
    swapped[-1] = (part, other)
    return jnp.concatenate([both(*pair) for pair in swapped[2:]]), grad_k


def score_tile(local_part, key_part, offset, tile_width, head_width):
    key_tile = lax.dynamic_slice_in_dim(key_part, offset, tile_width, 2)
    product = lax.dot_general(
        local_part, key_tile, (((1,), (1,)), ((0,), (0,))), preferred_element_type=jnp.float32
    )
    return product / math.sqrt(head_width)


def by_rows(teacher_q, teacher_k, student_in, w_query, w_key):
    query_width = DTQ // HEADS
    key_width = DTK // HEADS
    stud_width = DS // HEADS
    batch_count = teacher_q.shape[0]
    share = teacher_q.shape[1] // lax.axis_size("head")
    first = lax.axis_index("head") * share
    own_query = lax.dynamic_slice_in_dim(teacher_q, first, share, 1)
    own_key = lax.dynamic_slice_in_dim(teacher_k, first, share, 1)
    own_input = lax.dynamic_slice_in_dim(student_in, first, share, 1)
    teach_query, teach_key = (
        lax.all_to_all(
            own_query.transpose(2, 0, 1), "ctx", split_axis=0, concat_axis=2, tiled=True
        ),
        lax.all_to_all(own_key.transpose(2, 0, 1), "ctx", split_axis=0, concat_axis=2, tiled=True),
    )
    student_rows = lax.all_gather(own_input, "ctx", axis=1, tiled=True)
    row_count = student_rows.shape[1]
    across = (((1,), (2,)), ((), ()))
    stud_query = lax.dot_general(
        w_query, student_rows, across, preferred_element_type=jnp.float32
    ).astype(jnp.bfloat16)
    stud_key = lax.dot_general(
        w_key, student_rows, across, preferred_element_type=jnp.float32
    ).astype(jnp.bfloat16)
    heads_here = stud_query.shape[0] // stud_width
    gathered_all = (
        lax.all_gather(teach_query, "head", axis=2, tiled=True),
        lax.all_gather(teach_key, "head", axis=2, tiled=True),
        lax.all_gather(stud_query, "head", axis=2, tiled=True),
        lax.all_gather(stud_key, "head", axis=2, tiled=True),
    )
    own_all = (teach_query, teach_key, stud_query, stud_key)
    key_count = gathered_all[0].shape[2]
    widths = (query_width, key_width, stud_width, stud_width)
    tile_width = math.gcd(key_count, 512)
    tile_count = key_count // tile_width
    tiles = jnp.arange(tile_count)
    batched = (((2,), (2,)), ((0,), (0,)))
    weight_query = jnp.zeros((heads_here * stud_width, w_query.shape[1]), jnp.float32)
    weight_key = jnp.zeros((heads_here * stud_width, w_key.shape[1]), jnp.float32)
    for index in range(batch_count):
        local_parts = tuple(
            (
                own_all[member][:, index, :].reshape(heads_here, widths[member], row_count)
                for member in range(4)
            )
        )
        key_parts = tuple(
            (
                gathered_all[member][:, index, :].reshape(heads_here, widths[member], key_count)
                for member in range(4)
            )
        )

        def stat_step(state_now, tile_index):
            offset = tile_index * tile_width
            updated = []
            for member in range(4):
                running_max, running_sum = state_now[member]
                scores = score_tile(
                    local_parts[member], key_parts[member], offset, tile_width, widths[member]
                )
                new_max = jnp.maximum(running_max, jnp.max(scores, axis=2))
                running_sum = running_sum * jnp.exp(running_max - new_max) + jnp.sum(
                    jnp.exp(scores - new_max[:, :, None]), axis=2
                )
                updated.append((new_max, running_sum))
            return (tuple(updated), None)

        start_stats = tuple(
            (
                (
                    jnp.full((heads_here, row_count), -jnp.inf, jnp.float32),
                    jnp.zeros((heads_here, row_count), jnp.float32),
                )
                for member in range(4)
            )
        )
        final_stats, unused = lax.scan(stat_step, start_stats, tiles)
        log_totals = tuple(
            (final_stats[member][0] + jnp.log(final_stats[member][1]) for member in range(4))
        )
        zero_terms = jnp.zeros((heads_here, stud_width, row_count), jnp.float32)

        def grad_step(state_now, tile_index):
            offset = tile_index * tile_width
            scores = [
                score_tile(
                    local_parts[member], key_parts[member], offset, tile_width, widths[member]
                )
                for member in range(4)
            ]
            row_probs = [
                jnp.exp(scores[member] - log_totals[member][:, :, None]) for member in range(4)
            ]
            differences = (
                (row_probs[2] - row_probs[0]).astype(jnp.bfloat16),
                (row_probs[3] - row_probs[1]).astype(jnp.bfloat16),
            )
            key_tiles = (
                lax.dynamic_slice_in_dim(key_parts[2], offset, tile_width, 2),
                lax.dynamic_slice_in_dim(key_parts[3], offset, tile_width, 2),
            )
            row_terms = tuple(
                (
                    state_now[member]
                    + lax.dot_general(
                        key_tiles[member],
                        differences[member],
                        batched,
                        preferred_element_type=jnp.float32,
                    )
                    for member in range(2)
                )
            )
            contrib = tuple(
                (
                    lax.dot_general(
                        local_parts[2 + member],
                        differences[member],
                        (((2,), (1,)), ((0,), (0,))),
                        preferred_element_type=jnp.float32,
                    )
                    for member in range(2)
                )
            )
            return (row_terms, contrib)

        sums, pieces = lax.scan(grad_step, (zero_terms, zero_terms), tiles)
        row_query, row_key = sums
        spread = tuple(
            (
                pieces[member].transpose(1, 2, 0, 3).reshape(heads_here, stud_width, key_count)
                for member in range(2)
            )
        )
        col_query, col_key = (
            lax.psum_scatter(
                spread[0].astype(jnp.bfloat16), "head", scatter_dimension=2, tiled=True
            ).astype(jnp.float32),
            lax.psum_scatter(
                spread[1].astype(jnp.bfloat16), "head", scatter_dimension=2, tiled=True
            ).astype(jnp.float32),
        )
        query_grad = (
            ((row_query + col_query) / math.sqrt(stud_width))
            .astype(jnp.bfloat16)
            .reshape(heads_here * stud_width, row_count)
        )
        key_grad = (
            ((row_key + col_key) / math.sqrt(stud_width))
            .astype(jnp.bfloat16)
            .reshape(heads_here * stud_width, row_count)
        )
        weight_query = weight_query + lax.dot_general(
            query_grad,
            student_rows[index],
            (((1,), (0,)), ((), ())),
            preferred_element_type=jnp.float32,
        )
        weight_key = weight_key + lax.dot_general(
            key_grad,
            student_rows[index],
            (((1,), (0,)), ((), ())),
            preferred_element_type=jnp.float32,
        )
    grad_query, grad_key = (
        lax.psum(weight_query.astype(jnp.bfloat16), "head").astype(jnp.float32),
        lax.psum(weight_key.astype(jnp.bfloat16), "head").astype(jnp.float32),
    )
    return (grad_query, grad_key)


def solution(mesh):
    placed = (
        P(None, "ctx", None),
        P(None, "ctx", None),
        P(None, "ctx", None),
        P("ctx", None),
        P("ctx", None),
    )
    places = mesh.shape["ctx"]

    def on_device(*args):
        batch, tokens, _ = args[0].shape
        even = places in (8, 16, 32) and tokens % 32 == 0
        if even and batch == mesh.shape["head"] == 2 and tokens * places <= 1024:
            return by_sequence(*args)
        return by_rows(*args)

    return jax.shard_map(
        on_device,
        mesh=mesh,
        in_specs=placed,
        out_specs=(P("ctx", None), P("ctx", None)),
        check_vma=False,
    )
```
